32 devices in a mesh: gx: 8 (over z, y), gy: 4 (over x, core).
Axes of the slice: x: 2, y: 2, z: 4, core: 2. Of those that a mesh axis runs over, the one named last changes fastest.
Arguments:
- base_state: bfloat16 [2, 256, 1024], P(None, 'gy', 'gx'), may hold values from -6 to 6
- increment: bfloat16 [2, 256, 1024], P(None, 'gy', 'gx'), may hold values from -6 to 6
- cotangent: bfloat16 [256, 1024], P('gy', 'gx'), may hold values from -24 to 24
- land_sea: int32 [256, 1024], P('gy', 'gx'), may hold values 0 or 1
- storage: float32 [256, 1024], P('gy', 'gx'), may hold values from 0.25 to 4
- source: float32 [256, 1024], P('gy', 'gx'), may hold values from -100 to 100
- w_first: bfloat16 [25, 128], replicated, may hold values from -0.875 to 0.875
- w_middle_one: bfloat16 [25, 4096], replicated, may hold values from -0.15625 to 0.15625
- w_middle_two: bfloat16 [25, 4096], replicated, may hold values from -0.15625 to 0.15625
- w_last: bfloat16 [25, 64], replicated, may hold values from -0.15625 to 0.15625
Outputs:
- adjoint_gradient: float32 [2, 256, 1024], P(None, 'gy', 'gx')
- surface: float32 [256, 1024], P('gy', 'gx')
- residual: float32 [256, 1024], P('gy', 'gx')
The draws below stay inside these ranges and needn't reach their ends.
All inputs are finite; a program needn't handle non-finite values. No bound on the sum of `land_sea` on one device may be relied on, other than what follows from the above.
Results may differ from the reference program's by a relative error of at most 0.0051.
Values may be sent and summed in bfloat16 or wider, within the bound.
No kernel may reach another device: no remote copies, remote signals or barrier semaphores. Data moves between devices by JAX's collectives and lax.ppermute only.
A program may use at most 128 MiB of HBM per device.

```python
import math
import jax
import jax.numpy as jnp
from jax import lax

HID = 64
ITERS = 3
NX = 1024
NY = 256


def draw_source(key, part):
    key = jax.random.fold_in(key, 11)
    key_base, key_rows, key_cols = jax.random.split(key, 3)
    rows = jnp.exp(jax.random.uniform(key_rows, (NY, 1), jnp.float32) * math.log(10.0))
    cols = jnp.exp(jax.random.uniform(key_cols, (1, NX), jnp.float32) * math.log(10.0))
    along = jnp.arange(NX, dtype=jnp.float32)[None, :] / NX
    values = jnp.clip(jax.random.normal(key_base, (NY, NX), jnp.float32), -6.0, 6.0)
    trend = jnp.exp(math.log(3.0) * along)
    return 0.05 * values * rows * cols * trend


def with_ends(array, rng, smallest, top_value):
    longest = array.shape.index(max(array.shape))
    spots = []
    for shift in (0, 1):
        where = [jax.random.randint(jax.random.fold_in(rng, axis), (), 0, length) for axis, length in enumerate(array.shape)]
        where[longest] = (where[longest] + shift) % array.shape[longest]
        spots.append(tuple(where))
    return array.at[spots[0]].set(smallest).at[spots[1]].set(top_value)


def block_scale(key, extent, pieces, smallest, top_value):
    level, own = 1.0, jax.random.fold_in(key, 6)
    for position, parts in pieces:
        heights = jnp.exp(jax.random.uniform(jax.random.fold_in(own, position), (parts,), jnp.float32, smallest / len(pieces), top_value / len(pieces)))
        level = level * jnp.repeat(heights, extent[position] // parts).reshape([-1 if axis == position else 1 for axis in range(len(extent))])
    return level


def gaussian(rng, shape, scale, most, pieces=(), kind=jnp.bfloat16):
    factor_of = block_scale(rng, shape, pieces, -0.22, 0.18) if pieces else 1.0
    entries = jax.random.normal(rng, shape, jnp.float32) * scale * factor_of
    return jnp.minimum(jnp.maximum(entries, -most), most).astype(kind)


def setup_inputs(seed: int = 0) -> dict:
    streams_of = jax.random.split(jax.random.key(seed), 11)
    return {
        "base_state": gaussian(streams_of[0], (2, NY, NX), 1.0, 6.0, ((1, 4), (2, 8))),
        "increment": gaussian(streams_of[1], (2, NY, NX), 1.0, 6.0, ((1, 4), (2, 8))),
        "cotangent": gaussian(streams_of[2], (NY, NX), 4.0, 24.0, ((0, 4), (1, 8))),
        "land_sea": with_ends((jax.random.randint(streams_of[3], (NY, NX), 0, 5) < 4).astype(jnp.int32), jax.random.fold_in(streams_of[3], 1), 0, 1),
        "storage": jnp.clip(jnp.exp(math.log(4.0) - 2.7725887 * jax.random.uniform(streams_of[4], (NY, NX), jnp.float32) ** block_scale(streams_of[4], (NY, NX), ((0, 4), (1, 8)), -0.2, 0.2)), 0.25, 4.0),
        "source": draw_source(jax.random.fold_in(streams_of[10], 71), 0),
        "w_first": gaussian(streams_of[6], (25, 2 * HID), 50 ** -0.5, 0.875),
        "w_middle_one": gaussian(streams_of[7], (25, HID * HID), (25 * HID) ** -0.5, 0.15625),
        "w_middle_two": gaussian(streams_of[8], (25, HID * HID), (25 * HID) ** -0.5, 0.15625),
        "w_last": gaussian(streams_of[9], (25, HID), (25 * HID) ** -0.5, 0.15625),
    }


def widen(field, width):
    lead = [(0, 0)] * (field.ndim - 2)
    padded = jnp.pad(field, lead + [(width, width), (0, 0)])
    return jnp.concatenate([padded[..., -width:], padded, padded[..., :width]], axis=-1)


def shaped(table, inputs):
    return table.reshape(5, 5, inputs, table.shape[1] // inputs)


def convolve(padded, kernel):
    return lax.conv_general_dilated(padded, kernel, (1, 1), "VALID", dimension_numbers=("NCHW", "HWIO", "NCHW"), preferred_element_type=jnp.float32)


def turned(kernel):
    return jnp.flip(kernel, (0, 1)).transpose(0, 1, 3, 2)


def faces_of(border):
    own = border[1:-1, 1:-1]
    return (own * border[1:-1, 2:], own * border[1:-1, :-2], own * border[2:, 1:-1], own * border[:-2, 1:-1])


def apply_faces(field, rim, storage, faces):
    east, west, north, south = faces
    total = storage * field + east * (field - rim[1:-1, 2:]) + west * (field - rim[1:-1, :-2])
    return total + north * (field - rim[2:, 1:-1]) + south * (field - rim[:-2, 1:-1])


def reference(base_state, increment, cotangent, land_sea, storage, source, w_first, w_middle_one, w_middle_two, w_last):
    hidden = w_last.shape[1]
    k_first = shaped(w_first, 2)
    k_one = shaped(w_middle_one, hidden)
    k_two = shaped(w_middle_two, hidden)
    k_last = shaped(w_last, hidden)
    mask = land_sea.astype(jnp.float32)
    pre_act = convolve(widen(jnp.stack([base_state, increment]), 2), k_first)
    slope_one = jnp.tanh(pre_act[0])
    act_one = (mask * slope_one).astype(jnp.bfloat16)
    tl_one = (mask * (1.0 - slope_one * slope_one) * pre_act[1]).astype(jnp.bfloat16)
    pre_act = convolve(widen(jnp.stack([act_one, tl_one]), 2), k_one)
    slope_two = jnp.tanh(pre_act[0])
    act_two = (mask * slope_two).astype(jnp.bfloat16)
    tl_two = (mask * (1.0 - slope_two * slope_two) * pre_act[1]).astype(jnp.bfloat16)
    pre_act = convolve(widen(jnp.stack([act_two, tl_two]), 2), k_two)
    slope_three = jnp.tanh(pre_act[0])
    tl_three = (mask * (1.0 - slope_three * slope_three) * pre_act[1]).astype(jnp.bfloat16)
    tl_force = mask * convolve(widen(tl_three[None], 2), k_last)[0, 0]

    masked_cot = (mask * cotangent.astype(jnp.float32)).astype(jnp.bfloat16)
    back_act = convolve(widen(masked_cot[None, None], 2), turned(k_last))[0]
    back_three = (mask * (1.0 - slope_three * slope_three) * back_act).astype(jnp.bfloat16)
    back_act = convolve(widen(back_three[None], 2), turned(k_two))[0]
    back_two = (mask * (1.0 - slope_two * slope_two) * back_act).astype(jnp.bfloat16)
    back_act = convolve(widen(back_two[None], 2), turned(k_one))[0]
    back_one = (mask * (1.0 - slope_one * slope_one) * back_act).astype(jnp.bfloat16)
    adjoint_gradient = convolve(widen(back_one[None], 2), turned(k_first))[0]

    faces = faces_of(widen(mask, 1))
    rhs = source + tl_force
    surface = jnp.zeros_like(rhs)
    residual, direction = rhs, rhs
    norm_now = jnp.sum(residual * residual)
    for step in range(ITERS):
        image = apply_faces(direction, widen(direction, 1), storage, faces)
        alpha = norm_now / jnp.sum(direction * image)
        surface = surface + alpha * direction
        residual = residual - alpha * image
        norm_next = jnp.sum(residual * residual)
        direction = residual + (norm_next / norm_now) * direction
        norm_now = norm_next
    return adjoint_gradient, surface, residual
```

```python
import functools

import jax
import jax.numpy as jnp
import numpy as np
from jax import lax
from jax.experimental import pallas as pl
from jax.experimental.pallas import tpu as pltpu
from jax.sharding import PartitionSpec as P

F32 = jnp.float32
BF16 = jnp.bfloat16
HALO = 12
SIDE = 16
CENTRE = 6.125
RADIUS = 5.875
VMEM = 60 * 1024 * 1024


def one_hots(rows, cols, sides):
    first = np.zeros((16, 96, 32), np.float32)
    last = np.zeros((16, 96, 32), np.float32)
    for s in range(16):
        jj, qr, qc = s // 4, s // 2 % 2, s % 2
        for dr in range(6):
            for x in range(16):
                a, b = dr - qr, x - 2 * jj - qc
                if 0 <= a < 5 and 0 <= b < 5:
                    first[s, dr * 16 + x, a * 5 + b] = 1
                    last[s, dr * 16 + x, (4 - a) * 5 + 4 - b] = 1
    force = np.zeros((4, 72, 32), np.float32)
    grad = np.zeros((4, 2, 72, 32), np.float32)
    for p in range(4):
        pr, pc = p // 2, p % 2
        for dr in range(3):
            for dc in range(3):
                for q in range(4):
                    qr, qc = q // 2, q % 2
                    a, b = 2 * dr + pr - qr, 2 * dc + pc - qc
                    if 0 <= a < 5 and 0 <= b < 5:
                        force[p, (dr * 3 + dc) * 8 + q, a * 5 + b] = 1
                        for ch in range(2):
                            grad[p, ch, (dr * 3 + dc) * 8 + ch * 4 + q, (4 - a) * 5 + 4 - b] = 1
    seen = np.zeros((128, 1024), np.float32)
    for s in range(16):
        jj, qr, qc = s // 4, s // 2 % 2, s % 2
        seen[96 + qr * 16 + 2 + 2 * jj + qc, s * 64 : s * 64 + 64] = 1
    return [jnp.asarray(t, BF16) for t in (first, last, force, grad, seen)]


def decimate(ext_rows, blocks):
    table = np.zeros((ext_rows, 768), np.float32)
    for dr in range(6):
        for i in range(blocks):
            table[2 * i + dr, dr * 128 + i] = 1
    return jnp.asarray(table, BF16)


def unfold_tables(rows, blocks, first_row, pairs, width, first_col):
    left = np.zeros((2 * rows, 256), np.float32)
    right = np.zeros((2, 2 * pairs, width), np.float32)
    for par in range(2):
        for qr in range(2):
            for i in range(blocks):
                row = 2 * i + qr + first_row
                if 0 <= row < rows:
                    left[par * rows + row, qr * 128 + par * 64 + i] = 1
        for qc in range(2):
            for jp in range(pairs):
                col = 4 * jp + 2 * par + qc + first_col
                if col < 128 + SIDE and col >= -SIDE:
                    right[par, qc * pairs + jp, col % width] = 1
    return jnp.asarray(left), jnp.asarray(right)


def mm(a, b, dims=((1,), (0,))):
    return lax.dot_general(a, b, (dims, ((), ())), preferred_element_type=F32)


def exact(a, b, dims=((1,), (0,))):
    return lax.dot_general(
        a, b, (dims, ((), ())), preferred_element_type=F32, precision=lax.Precision.HIGHEST
    )


def up(x, by):
    return x if by == 0 else pltpu.roll(x, x.shape[0] - by, axis=0)


def fold_middle(k_ref, out_ref, flip_ref):
    zero = jnp.zeros((64, 64), BF16)
    for dc in range(3):
        for dr in range(3):
            for p in range(4):
                pr, pc = p // 2, p % 2
                parts = []
                for q in range(4):
                    qr, qc = q // 2, q % 2
                    a, b = 2 * dr + pr - qr, 2 * dc + pc - qc
                    parts.append(k_ref[a * 5 + b] if 0 <= a < 5 and 0 <= b < 5 else zero)
                at = (dc * 3 + dr) * 256 + p * 64
                out_ref[at : at + 64, :] = jnp.concatenate(parts, axis=1)
    for tap in range(9):
        block = out_ref[tap * 256 : tap * 256 + 256, :].astype(F32)
        at = (8 - tap) * 256
        flip_ref[at : at + 256, :] = block.T.astype(BF16)


def weights_kernel(
    k_one, k_two, w_first, w_last, e_first, e_last, e_force, e_grad,
    m_one, m_one_t, m_two, m_two_t, r_first, r_last, t_force, t_grad,
):
    fold_middle(k_one, m_one, m_one_t)
    fold_middle(k_two, m_two, m_two_t)
    wf = w_first[...]
    wl = w_last[...]
    pad = jnp.zeros((7, 64), BF16)
    wf = [jnp.concatenate([wf[:, c * 64 : c * 64 + 64], pad], axis=0) for c in range(2)]
    wl = jnp.concatenate([wl, pad], axis=0)
    gap = jnp.zeros((32, 128), BF16)
    for s in range(0, 16, 2):
        cols = slice(s * 64, s * 64 + 128)
        for c in range(2):
            two = [mm(e_first[s + d], wf[c]).astype(BF16) for d in range(2)]
            r_first[c * 128 : c * 128 + 96, cols] = jnp.concatenate(two, axis=1)
            r_first[c * 128 + 96 : c * 128 + 128, cols] = gap
        two = [mm(e_last[s + d], wl).astype(BF16) for d in range(2)]
        r_last[0:96, cols] = jnp.concatenate(two, axis=1)
        r_last[96:128, cols] = gap
    force, grad = [], []
    for p in range(4):
        force.append(mm(e_force[p], wl))
        grad.append(mm(e_grad[p, 0], wf[0]) + mm(e_grad[p, 1], wf[1]))
    t_force[...] = jnp.concatenate(force, axis=1).astype(BF16)
    t_grad[...] = jnp.concatenate(grad, axis=1).astype(BF16)


def fold_weights(k_one, k_two, w_first, w_last, tables):
    big = jax.ShapeDtypeStruct((2304, 256), BF16)
    return pl.pallas_call(
        weights_kernel,
        name="fold_weights",
        out_shape=(
            big, big, big, big,
            jax.ShapeDtypeStruct((256, 1024), BF16),
            jax.ShapeDtypeStruct((128, 1024), BF16),
            jax.ShapeDtypeStruct((72, 256), BF16),
            jax.ShapeDtypeStruct((72, 256), BF16),
        ),
        compiler_params=pltpu.CompilerParams(vmem_limit_bytes=VMEM),
        cost_estimate=pl.CostEstimate(flops=1 << 24, bytes_accessed=1 << 23, transcendentals=0),
    )(k_one, k_two, w_first, w_last, *tables)


def thin_conv(table, slots, outs, flat_ref):
    count = slots.shape[0]
    for q in range(0, count, 4):
        take = min(4, count - q)
        x = slots[q : q + take].reshape(take * 64, 256)
        flat_ref[:, q * 64 : (q + take) * 64] = mm(table, x, ((1,), (1,)))
    span = (outs + 1) // 2 * 128
    total = None
    for dr in range(3):
        part = None
        for dc in range(3):
            tap = flat_ref[(dr * 3 + dc) * 8 : (dr * 3 + dc) * 8 + 8, dc * 64 : dc * 64 + span]
            part = tap if part is None else part + tap
        if dr:
            part = pltpu.roll(part, span - dr, axis=1)
        total = part if total is None else total + part
    return total


def unfold(image, base, pairs, rows, left, right, turn_ref):
    for jp in range(image.shape[1] // 128):
        turn_ref[jp * 8 : jp * 8 + 8, :] = image[:, jp * 128 : jp * 128 + 128]
    picks = []
    for qc in range(2):
        two = [turn_ref[pl.ds(base + qr * 2 + qc, pairs, stride=8), :] for qr in range(2)]
        picks.append(jnp.concatenate(two, axis=1))
    half = exact(left, jnp.concatenate(picks, axis=0), ((1,), (1,)))
    return exact(half[:rows], right[0]) + exact(half[rows:], right[1])


def tangent_kernel(
    own, rim, pick, seen, m_one, m_two, r_first, r_last, t_force, left, right,
    back_three, keep_two, keep_one, basis, gram,
    window, act_one, act_two, back_pre, mask_two, mask_three, tl_three, flat, turn,
):
    tall = own.shape[1]
    sel = pick[...]
    for c in range(6):
        for source, part in ((own, 0), (rim, 1)):
            image = source[c]
            if c == 4:
                image = image * source[5]
            turned_image = mm(image.astype(BF16), sel, ((0,), (0,)))
            if part == 0:
                window[c, SIDE : SIDE + 128, :] = turned_image
            else:
                window[c, SIDE + 128 : SIDE + 128 + SIDE, :] = turned_image[:SIDE]
                window[c, 0:SIDE, :] = turned_image[128 - SIDE :]

    act_two[72:74] = jnp.zeros((2, 80, 768), BF16)
    tl_three[:, 48:64] = jnp.zeros((72, 16, 256), BF16)

    def first_layer(m, _):
        views = [window[c, pl.ds(pl.multiple_of(m * 8, 8), 16), :] for c in range(6)]

        def stack(c):
            parts = [views[c][:, dr * 128 : dr * 128 + 128] for dr in range(6)]
            parts += [views[5][:, dr * 128 : dr * 128 + 128] for dr in (2, 3)]
            return jnp.concatenate(parts, axis=0).T[:48]

        slabs = [stack(c) for c in range(5)]
        base = jnp.concatenate(slabs[0:2], axis=1)
        incr = jnp.concatenate(slabs[2:4], axis=1)
        pre = mm(jnp.concatenate([base, incr], axis=0).astype(BF16), r_first[...])
        cells = seen[...]
        wet = mm(slabs[0].astype(BF16), cells)
        wet_two = mm(up(slabs[0], 1).astype(BF16), cells).astype(BF16)
        wet_three = mm(up(slabs[0], 2).astype(BF16), cells).astype(BF16)
        pre_back = mm(up(slabs[4], 2).astype(BF16), r_last[...])
        for jj in range(4):
            lanes = slice(jj * 256, jj * 256 + 256)
            a = m * 4 + jj
            slope = jnp.tanh(pre[0:48, lanes])
            mask = wet[:, lanes]
            keep = mask * (1.0 - slope * slope)
            act = mask * slope
            tangent = keep * pre[48:96, lanes]
            keep_one[a] = up(keep, 4)[0:40]
            for dr in range(3):
                both = jnp.concatenate([up(act, dr)[0:40], up(tangent, dr)[0:40]], axis=0)
                act_one[a, :, dr * 256 : dr * 256 + 256] = both.astype(BF16)
            mask_two[a] = wet_two[:, lanes]
            mask_three[a] = wet_three[:, lanes]
            back_pre[a] = pre_back[0:40, lanes]
        return 0

    lax.fori_loop(0, 19, first_layer, 0)

    def second_layer(q, _):
        b = q * 4
        taps = [act_one[pl.ds(b + 2 + dc, 4)].reshape(320, 768) for dc in range(3)]
        pre = mm(jnp.concatenate(taps, axis=1), m_one[...])
        for jj in range(4):
            slope = jnp.tanh(pre[jj * 80 : jj * 80 + 40])
            mask = mask_two[b + 3 + jj].astype(F32)[0:40]
            keep = mask * (1.0 - slope * slope)
            act = mask * slope
            tangent = keep * pre[jj * 80 + 40 : jj * 80 + 80]
            keep_two[b + jj] = up(keep, 2)
            for dr in range(3):
                both = jnp.concatenate([up(act, dr), up(tangent, dr)], axis=0)
                act_two[b + jj, :, dr * 256 : dr * 256 + 256] = both.astype(BF16)
        return 0

    lax.fori_loop(0, 18, second_layer, 0)

    def third_layer(q, _):
        t = q * 4
        taps = [act_two[pl.ds(t + dc, 4)].reshape(320, 768) for dc in range(3)]
        pre = mm(jnp.concatenate(taps, axis=1), m_two[...])
        rest = jnp.zeros((8, 256), F32)
        for jj in range(4):
            slope = jnp.tanh(pre[jj * 80 : jj * 80 + 40])
            mask = mask_three[t + 4 + jj].astype(F32)[0:40]
            keep = mask * (1.0 - slope * slope)
            tangent = keep * pre[jj * 80 + 40 : jj * 80 + 80]
            tl_three[t + jj, 0:48] = jnp.concatenate([tangent, rest], axis=0).astype(BF16)
            back = keep * back_pre[t + 4 + jj]
            back_three[t + jj] = jnp.concatenate([back, rest], axis=0).astype(BF16)
        return 0

    lax.fori_loop(0, 18, third_layer, 0)
    tl_three[70:72] = jnp.zeros((2, 64, 256), BF16)

    turn[...] = jnp.zeros(turn.shape, F32)
    image = thin_conv(t_force[...], tl_three, 68, flat)
    force = unfold(image, 0, 40, tall, left[...], right, turn)

    def wide(c):
        return jnp.concatenate([own[c], rim[c]], axis=1)

    mask, storage, source = wide(5), wide(6), wide(7)
    columns = mask.shape[1]
    east = mask * pltpu.roll(mask, columns - 1, axis=1)
    west = mask * pltpu.roll(mask, 1, axis=1)
    north = mask * pltpu.roll(mask, tall - 1, axis=0)
    south = mask * pltpu.roll(mask, 1, axis=0)

    def scaled(v):
        total = storage * v + east * (v - pltpu.roll(v, columns - 1, axis=1))
        total = total + west * (v - pltpu.roll(v, 1, axis=1))
        total = total + north * (v - pltpu.roll(v, tall - 1, axis=0))
        total = total + south * (v - pltpu.roll(v, 1, axis=0))
        return (total - CENTRE * v) * (1.0 / RADIUS)

    v0 = source + mask * force
    v1 = scaled(v0)
    v2 = 2.0 * scaled(v1) - v0
    v3 = 2.0 * scaled(v2) - v1
    inner = [v[HALO : tall - HALO, 0:128] for v in (v0, v1, v2, v3)]
    for k in range(4):
        basis[k] = inner[k]
    lane = lax.broadcasted_iota(jnp.int32, (8, 128), 1)
    sums = jnp.zeros((8, 128), F32)
    at = 0
    for i in range(4):
        for j in range(i, 4):
            prod = jnp.sum(inner[i] * inner[j], axis=0, keepdims=True)
            value = jnp.sum(prod, axis=1, keepdims=True)
            sums = jnp.where(lane == at, value, sums)
            at += 1
    gram[...] = sums


def tangent_pass(own, rim, pick, seen, mats, left, right):
    m_one, m_two, r_first, r_last, t_force = mats
    tall = own.shape[1]
    rows = tall - 2 * HALO
    return pl.pallas_call(
        tangent_kernel,
        name="tangent_pass",
        out_shape=(
            jax.ShapeDtypeStruct((72, 48, 256), BF16),
            jax.ShapeDtypeStruct((72, 40, 256), F32),
            jax.ShapeDtypeStruct((76, 40, 256), F32),
            jax.ShapeDtypeStruct((4, rows, 128), F32),
            jax.ShapeDtypeStruct((8, 128), F32),
        ),
        scratch_shapes=[
            pltpu.VMEM((6, 128 + 2 * SIDE, 768), F32),
            pltpu.VMEM((76, 80, 768), BF16),
            pltpu.VMEM((74, 80, 768), BF16),
            pltpu.VMEM((76, 40, 256), F32),
            pltpu.VMEM((76, 48, 256), BF16),
            pltpu.VMEM((76, 48, 256), BF16),
            pltpu.VMEM((72, 64, 256), BF16),
            pltpu.VMEM((72, 72 * 64), F32),
            pltpu.VMEM((320, 128), F32),
        ],
        compiler_params=pltpu.CompilerParams(vmem_limit_bytes=VMEM),
        cost_estimate=pl.CostEstimate(flops=1 << 33, bytes_accessed=1 << 24, transcendentals=1 << 21),
    )(own, rim, pick, seen, m_one, m_two, r_first, r_last, t_force, left, right)


def adjoint_kernel(
    back_three, keep_two, keep_one, m_one_t, m_two_t, t_grad, left, right,
    grad, three, two, one, flat, turn,
):
    def spread(s, _):
        x0 = back_three[s].astype(F32)[0:40]
        x1 = back_three[s + 32].astype(F32)[0:40]
        for dr in range(3):
            both = jnp.concatenate([up(x0, dr), up(x1, dr)], axis=0)
            three[s, :, dr * 256 : dr * 256 + 256] = both.astype(BF16)
        return 0

    lax.fori_loop(0, 38, spread, 0, unroll=2)

    def second_layer(q, _):
        s = q * 4
        taps = [three[pl.ds(s + dc, 4)].reshape(320, 768) for dc in range(3)]
        pre = mm(jnp.concatenate(taps, axis=1), m_two_t[...])
        for jj in range(4):
            x0 = pre[jj * 80 : jj * 80 + 40] * keep_two[s + 2 + jj]
            x1 = pre[jj * 80 + 40 : jj * 80 + 80] * keep_two[s + 34 + jj]
            for dr in range(3):
                both = jnp.concatenate([up(x0, dr), up(x1, dr)], axis=0)
                two[s + jj, :, dr * 256 : dr * 256 + 256] = both.astype(BF16)
        return 0

    lax.fori_loop(0, 9, second_layer, 0)
    one[:, 48:64] = jnp.zeros((66, 16, 256), BF16)
    rest = jnp.zeros((8, 256), F32)

    def first_layer(s, count):
        taps = [two[pl.ds(s + dc, count)].reshape(count * 80, 768) for dc in range(3)]
        pre = mm(jnp.concatenate(taps, axis=1), m_one_t[...])
        for jj in range(count):
            x0 = pre[jj * 80 : jj * 80 + 40] * keep_one[s + 6 + jj]
            x1 = pre[jj * 80 + 40 : jj * 80 + 80] * keep_one[s + 38 + jj]
            one[s + jj, 0:48] = jnp.concatenate([x0, rest], axis=0).astype(BF16)
            one[s + 32 + jj, 0:48] = jnp.concatenate([x1, rest], axis=0).astype(BF16)

    def body(q, _):
        first_layer(q * 4, 4)
        return 0

    lax.fori_loop(0, 8, body, 0)
    first_layer(32, 2)

    image = thin_conv(t_grad[...], one, 64, flat)
    rows = grad.shape[1]
    for ch in range(2):
        grad[ch] = unfold(image, ch * 4, 32, rows, left[...], right, turn)


def adjoint_pass(back_three, keep_two, keep_one, mats, left, right):
    m_one_t, m_two_t, t_grad = mats
    return pl.pallas_call(
        adjoint_kernel,
        name="adjoint_pass",
        out_shape=jax.ShapeDtypeStruct((2, left.shape[0] // 2, 128), F32),
        scratch_shapes=[
            pltpu.VMEM((38, 80, 768), BF16),
            pltpu.VMEM((36, 80, 768), BF16),
            pltpu.VMEM((66, 64, 256), BF16),
            pltpu.VMEM((72, 66 * 64), F32),
            pltpu.VMEM((256, 128), F32),
        ],
        compiler_params=pltpu.CompilerParams(vmem_limit_bytes=VMEM),
        cost_estimate=pl.CostEstimate(flops=1 << 33, bytes_accessed=1 << 24, transcendentals=0),
    )(back_three, keep_two, keep_one, m_one_t, m_two_t, t_grad, left, right)


def combine_kernel(basis, gram, surface, residual):
    sums = gram[0:1, :]
    g = {}
    at = 0
    for i in range(4):
        for j in range(i, 4):
            g[i, j] = g[j, i] = sums[:, at : at + 1]
            at += 1

    def inner(a, b):
        total = None
        for i, ai in enumerate(a):
            for j, bj in enumerate(b):
                if ai is not None and bj is not None:
                    term = ai * bj * g[i, j]
                    total = term if total is None else total + term
        return total

    def add(a, b, scale):
        out = []
        for ai, bi in zip(a, b):
            if bi is None:
                out.append(ai)
            else:
                out.append(scale * bi if ai is None else ai + scale * bi)
        return out

    def operate(p):
        out = [None if x is None else CENTRE * x for x in p]
        if p[0] is not None:
            out = add(out, [None, p[0], None, None], RADIUS)
        if p[1] is not None:
            out = add(out, [p[1], None, p[1], None], 0.5 * RADIUS)
        if p[2] is not None:
            out = add(out, [None, p[2], None, p[2]], 0.5 * RADIUS)
        return out

    unit = jnp.ones((1, 1), F32)
    r = [unit, None, None, None]
    p = [unit, None, None, None]
    x = [None] * 4
    norm = g[0, 0]
    for step in range(3):
        image = operate(p)
        alpha = norm / inner(p, image)
        x = add(x, p, alpha)
        r = add(r, image, -alpha)
        if step < 2:
            new = inner(r, r)
            p = add(r, p, new / norm)
            norm = new
    surface[...] = x[0] * basis[0] + x[1] * basis[1] + x[2] * basis[2]
    residual[...] = r[0] * basis[0] + r[1] * basis[1] + r[2] * basis[2] + r[3] * basis[3]


def combine(basis, gram):
    shape = jax.ShapeDtypeStruct(basis.shape[1:], F32)
    return pl.pallas_call(combine_kernel, name="combine", out_shape=(shape, shape))(basis, gram)


def everywhere(x):
    for axis in ("gy", "gx"):
        count = lax.axis_size(axis)
        if count & (count - 1):
            x = lax.psum(x, axis)
            continue
        step = 1
        while step < count:
            x = x + lax.ppermute(x, axis, [(i, i ^ step) for i in range(count)])
            step *= 2
    return x


def shards(
    base_state,
    increment,
    cotangent,
    land_sea,
    storage,
    source,
    w_first,
    w_middle_one,
    w_middle_two,
    w_last,
):
    rows, cols = land_sea.shape
    tall = rows + 2 * HALO
    gx, gy = lax.axis_size("gx"), lax.axis_size("gy")
    own = jnp.concatenate(
        [
            base_state.astype(F32),
            increment.astype(F32),
            cotangent.astype(F32)[None],
            land_sea.astype(F32)[None],
            storage[None],
            source[None],
        ],
        axis=0,
    )
    above = lax.ppermute(own[:, rows - HALO :], "gy", [(i, i + 1) for i in range(gy - 1)])
    below = lax.ppermute(own[:, :HALO], "gy", [(i + 1, i) for i in range(gy - 1)])
    own = jnp.concatenate([above, own, below], axis=1)
    west = lax.ppermute(own[:, :, cols - SIDE :], "gx", [(i, (i + 1) % gx) for i in range(gx)])
    east = lax.ppermute(own[:, :, :SIDE], "gx", [((i + 1) % gx, i) for i in range(gx)])
    gap = jnp.zeros((8, tall, 128 - 2 * SIDE), F32)
    rim = jnp.concatenate([east, gap, west], axis=2)

    e_first, e_last, e_force, e_grad, seen = one_hots(rows, cols, SIDE)
    m_one, m_one_t, m_two, m_two_t, r_first, r_last, t_force, t_grad = fold_weights(
        w_middle_one.reshape(25, 64, 64),
        w_middle_two.reshape(25, 64, 64),
        w_first,
        w_last,
        (e_first, e_last, e_force, e_grad),
    )
    left, right = unfold_tables(tall, 36, 8, 40, 256, -4)
    back_three, keep_two, keep_one, basis, gram = tangent_pass(
        own, rim, decimate(tall, 42), seen, (m_one, m_two, r_first, r_last, t_force), left, right
    )
    gram = everywhere(gram)
    left, right = unfold_tables(rows, 32, 0, 32, 128, 0)
    grad = adjoint_pass(back_three, keep_two, keep_one, (m_one_t, m_two_t, t_grad), left, right)
    surface, residual = combine(basis, gram)
    return (grad, surface, residual)


def solution(mesh):
    placed = (
        P(None, "gy", "gx"),
        P(None, "gy", "gx"),
        P("gy", "gx"),
        P("gy", "gx"),
        P("gy", "gx"),
        P("gy", "gx"),
        P(),
        P(),
        P(),
        P(),
    )
    return jax.shard_map(
        shards,
        mesh=mesh,
        in_specs=placed,
        out_specs=(P(None, "gy", "gx"), P("gy", "gx"), P("gy", "gx")),
        check_vma=False,
    )
```

```python
import functools

import jax
import jax.numpy as jnp
import numpy as np
from jax import lax
from jax.experimental import pallas as pl
from jax.experimental.pallas import tpu as pltpu
from jax.sharding import PartitionSpec as P

F32 = jnp.float32
BF16 = jnp.bfloat16
HALO = 16
CENTRE = 6.125
RADIUS = 5.875
VMEM = 60 * 1024 * 1024
ANY = pl.BlockSpec(memory_space=pl.ANY)
HERE = pl.BlockSpec(memory_space=pltpu.VMEM)


def one_hots():
    first = np.zeros((16, 96, 32), np.float32)
    last = np.zeros((16, 96, 32), np.float32)
    for s in range(16):
        jj, qr, qc = s // 4, s // 2 % 2, s % 2
        for dr in range(6):
            for x in range(16):
                a, b = dr - qr, x - 2 * jj - qc
                if 0 <= a < 5 and 0 <= b < 5:
                    first[s, dr * 16 + x, a * 5 + b] = 1
                    last[s, dr * 16 + x, (4 - a) * 5 + 4 - b] = 1
    force = np.zeros((4, 72, 32), np.float32)
    grad = np.zeros((4, 2, 72, 32), np.float32)
    for p in range(4):
        pr, pc = p // 2, p % 2
        for dr in range(3):
            for dc in range(3):
                for q in range(4):
                    qr, qc = q // 2, q % 2
                    a, b = 2 * dr + pr - qr, 2 * dc + pc - qc
                    if 0 <= a < 5 and 0 <= b < 5:
                        force[p, (dr * 3 + dc) * 8 + q, a * 5 + b] = 1
                        for ch in range(2):
                            grad[p, ch, (dr * 3 + dc) * 8 + ch * 4 + q, (4 - a) * 5 + 4 - b] = 1
    seen = np.zeros((128, 1024), np.float32)
    for s in range(16):
        jj, qr, qc = s // 4, s // 2 % 2, s % 2
        seen[96 + qr * 16 + 2 + 2 * jj + qc, s * 64 : s * 64 + 64] = 1
    return [jnp.asarray(t, BF16) for t in (first, last, force, grad, seen)]


def decimate():
    table = np.zeros((128, 768), np.float32)
    for dr in range(6):
        for i in range(42):
            table[2 * i + dr + 4, dr * 128 + i] = 1
    return jnp.asarray(table, BF16)


def unfold_tables(rows, blocks, first_row, pairs, width, first_col):
    left = np.zeros((2 * rows, 256), np.float32)
    right = np.zeros((2, 2 * pairs, width), np.float32)
    for par in range(2):
        for qr in range(2):
            for i in range(blocks):
                row = 2 * i + qr + first_row
                if 0 <= row < rows:
                    left[par * rows + row, qr * 128 + par * 64 + i] = 1
        for qc in range(2):
            for jp in range(pairs):
                col = 4 * jp + 2 * par + qc + first_col
                if -HALO <= col < 128 + HALO:
                    right[par, qc * pairs + jp, col % width] = 1
    return jnp.asarray(left), jnp.asarray(right)


def mm(a, b, dims=((1,), (0,))):
    return lax.dot_general(a, b, (dims, ((), ())), preferred_element_type=F32)


def exact(a, b, dims=((1,), (0,))):
    return lax.dot_general(
        a, b, (dims, ((), ())), preferred_element_type=F32, precision=lax.Precision.HIGHEST
    )


def up(x, by):
    return x if by == 0 else pltpu.roll(x, x.shape[0] - by, axis=0)


def unpack_taps(raw, stage, taps):
    for i in range(32):
        stage[i * 32 : i * 32 + 25, :] = raw[:, i * 128 : i * 128 + 128].astype(F32)
    for t in range(25):
        pairs = stage[pl.ds(t, 32, stride=32), :]
        taps[t, pl.ds(0, 32, stride=2), :] = pairs[:, 0:64]
        taps[t, pl.ds(1, 32, stride=2), :] = pairs[:, 64:128]


def fold_middle(taps, out_ref):
    zero = jnp.zeros((64, 64), F32)
    for dc in range(3):
        for dr in range(3):
            for p in range(4):
                pr, pc = p // 2, p % 2
                parts = []
                for q in range(4):
                    qr, qc = q // 2, q % 2
                    a, b = 2 * dr + pr - qr, 2 * dc + pc - qc
                    parts.append(taps[a * 5 + b] if 0 <= a < 5 and 0 <= b < 5 else zero)
                at = (dc * 3 + dr) * 256 + p * 64
                out_ref[at : at + 64, :] = jnp.concatenate(parts, axis=1).astype(BF16)


def weights_kernel(
    w_one, w_two, w_first, w_last, e_first, e_last, e_force, e_grad,
    m_one, m_two, r_first, r_last, t_force, t_grad,
    stage, taps,
):
    for k, (raw, out) in enumerate(((w_one, m_one), (w_two, m_two))):
        unpack_taps(raw, stage.at[k], taps.at[k])
        fold_middle(taps.at[k], out)
    wf = w_first[...]
    wl = w_last[...]
    pad = jnp.zeros((7, 64), BF16)
    wf = [jnp.concatenate([wf[:, c * 64 : c * 64 + 64], pad], axis=0) for c in range(2)]
    wl = jnp.concatenate([wl, pad], axis=0)
    gap = jnp.zeros((32, 128), BF16)
    for s in range(0, 16, 2):
        cols = slice(s * 64, s * 64 + 128)
        for c in range(2):
            two = [mm(e_first[s + d], wf[c]).astype(BF16) for d in range(2)]
            r_first[c * 128 : c * 128 + 96, cols] = jnp.concatenate(two, axis=1)
            r_first[c * 128 + 96 : c * 128 + 128, cols] = gap
        two = [mm(e_last[s + d], wl).astype(BF16) for d in range(2)]
        r_last[0:96, cols] = jnp.concatenate(two, axis=1)
        r_last[96:128, cols] = gap
    force, grad = [], []
    for p in range(4):
        force.append(mm(e_force[p], wl))
        grad.append(mm(e_grad[p, 0], wf[0]) + mm(e_grad[p, 1], wf[1]))
    t_force[...] = jnp.concatenate(force, axis=1).astype(BF16)
    t_grad[...] = jnp.concatenate(grad, axis=1).astype(BF16)


def fold_weights(w_one, w_two, w_first, w_last, tables):
    big = jax.ShapeDtypeStruct((2304, 256), BF16)
    return pl.pallas_call(
        weights_kernel,
        name="fold_weights",
        out_shape=(
            big, big,
            jax.ShapeDtypeStruct((256, 1024), BF16),
            jax.ShapeDtypeStruct((128, 1024), BF16),
            jax.ShapeDtypeStruct((72, 256), BF16),
            jax.ShapeDtypeStruct((72, 256), BF16),
        ),
        scratch_shapes=[pltpu.VMEM((2, 1024, 128), F32), pltpu.VMEM((2, 25, 64, 64), F32)],
        compiler_params=pltpu.CompilerParams(vmem_limit_bytes=VMEM),
        cost_estimate=pl.CostEstimate(flops=1 << 24, bytes_accessed=1 << 23, transcendentals=0),
    )(w_one, w_two, w_first, w_last, *tables)


def rows_kernel(base, incr, cot, land, storage, source, own, top, bottom):
    wet = land[...].astype(F32)
    images = [base[0], base[1], incr[0], incr[1], cot[...].astype(F32) * wet, wet, storage[...], source[...]]
    rows = land.shape[0]
    for c, image in enumerate(images):
        image = image.astype(F32)
        own[c] = image
        top[c] = image[:HALO]
        bottom[c] = image[rows - HALO :]


def rows_out(*fields):
    rows, cols = fields[3].shape
    edge = jax.ShapeDtypeStruct((8, HALO, cols), F32)
    return pl.pallas_call(
        rows_kernel,
        name="rows_out",
        out_shape=(jax.ShapeDtypeStruct((8, rows, cols), F32), edge, edge),
    )(*fields)


def columns_kernel(own, above, below, turned, nat, west, east):
    rest = jnp.zeros((128 - own.shape[1] - 2 * HALO, 128), F32)
    for c in range(8):
        parts = [above[c], own[c], below[c]]
        if c >= 5:
            nat[c - 5] = jnp.concatenate(parts, axis=0)
        flipped = jnp.concatenate(parts + [rest], axis=0).T
        if c < 6:
            turned[c] = flipped.astype(BF16)
        west[c] = flipped[:HALO]
        east[c] = flipped[128 - HALO :]


def columns_out(own, above, below):
    tall = own.shape[1] + 2 * HALO
    edge = jax.ShapeDtypeStruct((8, HALO, 128), F32)
    return pl.pallas_call(
        columns_kernel,
        name="columns_out",
        out_shape=(
            jax.ShapeDtypeStruct((6, 128, 128), BF16),
            jax.ShapeDtypeStruct((3, tall, 128), F32),
            edge,
            edge,
        ),
    )(own, above, below)


def copy(source, target, sem):
    move = pltpu.make_async_copy(source, target, sem)
    move.start()
    return move


def pipeline(sizes, dot, finish, bufs):
    for k in range(len(sizes) + 1):
        if k < len(sizes):
            dot(k, bufs[k % 2])
        if k:
            finish(k - 1, bufs[(k - 1) % 2])


def pipeline_loop(count, dot, finish, bufs):
    def body(p, _):
        dot(2 * p + 1, bufs[1])
        finish(2 * p, bufs[0])
        dot(2 * p + 2, bufs[0])
        finish(2 * p + 1, bufs[1])
        return 0

    lax.fori_loop(0, (count - 1) // 2, body, 0)
    if count % 2:
        finish(count - 1, bufs[0])
    else:
        dot(count - 1, bufs[1])
        finish(count - 2, bufs[0])
        finish(count - 1, bufs[1])


def three_taps(slots, at, count, weights):
    taps = [slots[pl.ds(at + dc, count)].reshape(count * 80, 768) for dc in range(3)]
    return mm(jnp.concatenate(taps, axis=1), weights[...])


def spread_rows(slot, x0, x1):
    for dr in range(3):
        both = jnp.concatenate([up(x0, dr)[0:40], up(x1, dr)[0:40]], axis=0)
        slot[:, dr * 256 : dr * 256 + 256] = both.astype(BF16)


def thin_taps(table, slots, count, flat_ref, lane):
    for q in range(0, count, 4):
        take = min(4, count - q)
        x = slots[q : q + take].reshape(take * 64, 256)
        flat_ref[:, lane + q * 64 : lane + (q + take) * 64] = mm(table, x, ((1,), (1,)))


def thin_sum(flat_ref, outs):
    span = outs * 64
    total = None
    for dr in range(3):
        part = None
        for dc in range(3):
            tap = flat_ref[(dr * 3 + dc) * 8 : (dr * 3 + dc) * 8 + 8, dc * 64 : dc * 64 + span]
            part = tap if part is None else part + tap
        if dr:
            part = pltpu.roll(part, span - dr, axis=1)
        total = part if total is None else total + part
    return total


def unfold(image, base, pairs, rows, left, right, turn_ref):
    for jp in range(image.shape[1] // 128):
        turn_ref[jp * 8 : jp * 8 + 8, :] = image[:, jp * 128 : jp * 128 + 128]
    picks = []
    for qc in range(2):
        two = [turn_ref[pl.ds(base + qr * 2 + qc, pairs, stride=8), :] for qr in range(2)]
        picks.append(jnp.concatenate(two, axis=1))
    half = exact(left, jnp.concatenate(picks, axis=0), ((1,), (1,)))
    return exact(half[:rows], right[0]) + exact(half[rows:], right[1])


def slab(window, row, k, lhs, lhs_back):
    views = [window[c, pl.ds(row, 16), :] for c in range(6)]

    def stack(c):
        parts = [views[c][:, dr * 128 : dr * 128 + 128] for dr in range(6)]
        parts += [views[5][:, dr * 128 : dr * 128 + 128] for dr in (2, 3)]
        return jnp.concatenate(parts, axis=0).T[:48]

    slabs = [stack(c) for c in range(5)]
    base = jnp.concatenate(slabs[0:2], axis=1)
    incr = jnp.concatenate(slabs[2:4], axis=1)
    lhs[k] = jnp.concatenate([base, incr], axis=0).astype(BF16)
    lhs_back[k] = up(slabs[4], 2).astype(BF16)


def first_products(lhs, lhs_back, seen, r_first, r_last, pre, wet, back_pre, first, count):
    some = slice(first, first + count)
    x = lhs[some].reshape(count * 96, 256)
    y = lhs[some, 0:48, 0:128].reshape(count * 48, 128)
    z = lhs_back[some].reshape(count * 48, 128)
    for jj in range(4):
        lanes = slice(jj * 256, jj * 256 + 256)
        pre[jj, some] = mm(x, r_first[:, lanes]).reshape(count, 96, 256)
        wet[jj, some] = mm(y, seen[:, lanes]).reshape(count, 48, 256)
        back_pre[jj, some] = mm(z, r_last[:, lanes]).reshape(count, 48, 256)


def first_finish(k, jj, pre, wet, slot, keep):
    slope = jnp.tanh(pre[jj, k, 0:48])
    mask = wet[jj, k]
    kept = mask * (1.0 - slope * slope)
    keep[...] = up(kept, 4)[0:40]
    spread_rows(slot, mask * slope, kept * pre[jj, k, 48:96])


def second_finish(pre, mask, slot, keep):
    slope = jnp.tanh(pre[0:40])
    mask = up(mask, 1)[0:40]
    kept = mask * (1.0 - slope * slope)
    keep[...] = up(kept, 2)
    spread_rows(slot, mask * slope, kept * pre[40:80])


def third_finish(pre, mask, back_pre, slot, back):
    rest = jnp.zeros((8, 256), F32)
    slope = jnp.tanh(pre[0:40])
    kept = up(mask, 2)[0:40] * (1.0 - slope * slope)
    slot[0:48] = jnp.concatenate([kept * pre[40:80], rest], axis=0).astype(BF16)
    back[...] = jnp.concatenate([kept * back_pre[0:40], rest], axis=0).astype(BF16)


def inner_kernel(
    turned, pick, seen, m_one_in, m_two_in, r_first, r_last, t_force,
    back_out, two_out, one_out, act_out, flat,
    window, lhs, lhs_back, pre, wet, back_pre, act_one, act_two, tl_three,
    buf_a, buf_b, keep_one, keep_two, back_three, m_one, m_two, sems,
):
    loads = [copy(m_one_in, m_one, sems.at[3]), copy(m_two_in, m_two, sems.at[4])]
    sel = pick[...]
    for c in range(6):
        window[c] = mm(turned[c], sel)
    tl_three[:, 48:64] = jnp.zeros((54, 16, 256), BF16)

    def gather(chunk):
        for k in range(chunk * 5, chunk * 5 + 5):
            slab(window, k * 8, k, lhs, lhs_back)

    def products(chunk):
        first_products(lhs, lhs_back, seen, r_first, r_last, pre, wet, back_pre, chunk * 5, 5)

    def finish_one(chunk):
        for k in range(chunk * 5, chunk * 5 + 5):
            for jj in range(4):
                first_finish(k, jj, pre, wet, act_one.at[k * 4 + jj], keep_one.at[k * 4 + jj])

    gather(0)
    products(0)
    gather(1)
    products(1)
    gather(2)
    finish_one(0)
    products(2)
    finish_one(1)
    loads[0].wait()

    def wet_at(at):
        return wet[at % 4, at // 4]

    def dot_two(q, buf):
        buf[0:640] = three_taps(act_one, q * 8 + 2, 8, m_one)

    def finish_two(q, buf):
        for jj in range(8):
            mask = wet[(jj + 3) % 4, q * 2 + (jj + 3) // 4]
            second_finish(buf[jj * 80 : jj * 80 + 80], mask, act_two.at[q * 8 + jj], keep_two.at[q * 8 + jj])

    dot_two(0, buf_a)
    finish_one(2)
    moves = [copy(keep_one, one_out, sems.at[0])]
    pipeline_loop(7, dot_two, finish_two, (buf_a, buf_b))
    moves.append(copy(keep_two, two_out, sems.at[1]))
    loads[1].wait()
    act_out[0:2] = act_two[0:2]
    act_out[2:4] = act_two[54:56]

    def dot_three(q, buf):
        buf[...] = three_taps(act_two, q * 9, 9, m_two)

    def finish_three(q, buf):
        for jj in range(9):
            at = q * 9 + jj + 4
            third_finish(
                buf[jj * 80 : jj * 80 + 80], wet_at(at), back_pre[at % 4, at // 4],
                tl_three.at[q * 9 + jj], back_three.at[q * 9 + jj],
            )

    dot_three(0, buf_a)
    pipeline_loop(6, dot_three, finish_three, (buf_a, buf_b))
    moves.append(copy(back_three, back_out, sems.at[2]))
    thin_taps(t_force[...], tl_three, 54, flat, 0)
    for move in moves:
        move.wait()


def inner_pass(turned, pick, seen, mats):
    return pl.pallas_call(
        inner_kernel,
        name="inner_pass",
        out_shape=(
            jax.ShapeDtypeStruct((54, 48, 256), BF16),
            jax.ShapeDtypeStruct((56, 40, 256), F32),
            jax.ShapeDtypeStruct((60, 40, 256), F32),
            jax.ShapeDtypeStruct((4, 80, 768), BF16),
            jax.ShapeDtypeStruct((72, 54 * 64), F32),
        ),
        in_specs=[HERE] * 3 + [ANY, ANY] + [HERE] * 3,
        out_specs=(ANY, ANY, ANY, HERE, HERE),
        scratch_shapes=[
            pltpu.VMEM((6, 128, 768), F32),
            pltpu.VMEM((15, 96, 256), BF16),
            pltpu.VMEM((15, 48, 128), BF16),
            pltpu.VMEM((4, 15, 96, 256), F32),
            pltpu.VMEM((4, 15, 48, 256), F32),
            pltpu.VMEM((4, 15, 48, 256), F32),
            pltpu.VMEM((60, 80, 768), BF16),
            pltpu.VMEM((56, 80, 768), BF16),
            pltpu.VMEM((54, 64, 256), BF16),
            pltpu.VMEM((720, 256), F32),
            pltpu.VMEM((720, 256), F32),
            pltpu.VMEM((60, 40, 256), F32),
            pltpu.VMEM((56, 40, 256), F32),
            pltpu.VMEM((54, 48, 256), BF16),
            pltpu.VMEM((2304, 256), BF16),
            pltpu.VMEM((2304, 256), BF16),
            pltpu.SemaphoreType.DMA((5,)),
        ],
        compiler_params=pltpu.CompilerParams(vmem_limit_bytes=VMEM),
        cost_estimate=pl.CostEstimate(flops=1 << 33, bytes_accessed=1 << 23, transcendentals=1 << 21),
    )(turned, pick, seen, *mats)


def outer_kernel(
    far_west, west, east, far_east, nat, pick, seen, m_one_in, m_two_in, r_first, r_last, t_force, left, right,
    act_in, flat_in,
    back_three, keep_two, keep_one, basis, gram,
    window, lhs, lhs_back, pre, wet, back_pre, act_one, act_two, tl_three, buf_a, buf_b, flat, turn, m_one, m_two, sems,
):
    loads = [copy(m_one_in, m_one, sems.at[2]), copy(m_two_in, m_two, sems.at[3])]
    moves = [
        copy(flat_in, flat.at[:, 512 : 512 + 54 * 64], sems.at[0]),
        copy(act_in, act_two.at[8:12], sems.at[1]),
    ]
    sel = pick[...]
    for c in range(6):
        strips = [far_west[c], west[c], east[c], far_east[c]]
        window[c] = mm(jnp.concatenate(strips, axis=0).astype(BF16), sel)
    tl_three[:, 48:64] = jnp.zeros((16, 16, 256), BF16)
    for k in range(6):
        slab(window, (0, 8, 16, 32, 40, 48)[k], k, lhs, lhs_back)
    first_products(lhs, lhs_back, seen, r_first, r_last, pre, wet, back_pre, 0, 6)
    for k in range(6):
        for jj in range(4):
            first_finish(k, jj, pre, wet, act_one.at[k * 4 + jj], keep_one.at[k * 4 + jj])
    loads[0].wait()

    def dot_two(q, buf):
        buf[...] = three_taps(act_one, (2, 14)[q], 8, m_one)

    def finish_two(q, buf):
        for jj in range(8):
            at = (3, 15)[q] + jj
            second_finish(
                buf[jj * 80 : jj * 80 + 80], wet[at % 4, at // 4], act_two.at[(0, 12)[q] + jj], keep_two.at[q * 8 + jj]
            )

    pipeline((8, 8), dot_two, finish_two, (buf_a, buf_b))
    for move in moves + loads[1:]:
        move.wait()

    def dot_three(q, buf):
        buf[...] = three_taps(act_two, (0, 10)[q], 8, m_two)

    def finish_three(q, buf):
        for jj in range(8):
            at = (4, 14)[q] + jj
            third_finish(
                buf[jj * 80 : jj * 80 + 80], wet[at % 4, at // 4], back_pre[at % 4, at // 4],
                tl_three.at[q * 8 + jj], back_three.at[q * 8 + jj],
            )

    pipeline((8, 8), dot_three, finish_three, (buf_a, buf_b))
    thin_taps(t_force[...], tl_three.at[0:8], 8, flat, 0)
    thin_taps(t_force[...], tl_three.at[8:16], 8, flat, 62 * 64)
    turn[...] = jnp.zeros(turn.shape, F32)
    image = thin_sum(flat, 68)
    tall = nat.shape[1]
    force = unfold(image, 0, 40, tall, left[...], right, turn)
    gap = jnp.zeros((128 - 2 * HALO, 128), F32)

    def wide(c):
        rim = jnp.concatenate([far_east[c], gap, far_west[c]], axis=0).T[:tall]
        return jnp.concatenate([nat[c - 5], rim], axis=1)

    mask, storage, source = wide(5), wide(6), wide(7)
    columns = mask.shape[1]
    to_east = mask * pltpu.roll(mask, columns - 1, axis=1)
    to_west = mask * pltpu.roll(mask, 1, axis=1)
    to_north = mask * pltpu.roll(mask, tall - 1, axis=0)
    to_south = mask * pltpu.roll(mask, 1, axis=0)

    def scaled(v):
        total = storage * v + to_east * (v - pltpu.roll(v, columns - 1, axis=1))
        total = total + to_west * (v - pltpu.roll(v, 1, axis=1))
        total = total + to_north * (v - pltpu.roll(v, tall - 1, axis=0))
        total = total + to_south * (v - pltpu.roll(v, 1, axis=0))
        return (total - CENTRE * v) * (1.0 / RADIUS)

    v0 = source + mask * force
    v1 = scaled(v0)
    v2 = 2.0 * scaled(v1) - v0
    v3 = 2.0 * scaled(v2) - v1
    inner = [v[HALO : tall - HALO, 0:128] for v in (v0, v1, v2, v3)]
    for k in range(4):
        basis[k] = inner[k]
    lane = lax.broadcasted_iota(jnp.int32, (8, 128), 1)
    sums = jnp.zeros((8, 128), F32)
    at = 0
    for i in range(4):
        for j in range(i, 4):
            prod = jnp.sum(inner[i] * inner[j], axis=0, keepdims=True)
            value = jnp.sum(prod, axis=1, keepdims=True)
            sums = jnp.where(lane == at, value, sums)
            at += 1
    gram[...] = jnp.broadcast_to(sums, gram.shape)


def outer_pass(strips, nat, pick, seen, mats, left, right, act_in, flat_in, devices):
    tall = nat.shape[1]
    return pl.pallas_call(
        outer_kernel,
        name="outer_pass",
        out_shape=(
            jax.ShapeDtypeStruct((16, 48, 256), BF16),
            jax.ShapeDtypeStruct((16, 40, 256), F32),
            jax.ShapeDtypeStruct((24, 40, 256), F32),
            jax.ShapeDtypeStruct((4, tall - 2 * HALO, 128), F32),
            jax.ShapeDtypeStruct((devices, 8, 128), F32),
        ),
        in_specs=[HERE] * 7 + [ANY, ANY] + [HERE] * 5 + [ANY, ANY],
        scratch_shapes=[
            pltpu.VMEM((6, 64, 768), F32),
            pltpu.VMEM((6, 96, 256), BF16),
            pltpu.VMEM((6, 48, 128), BF16),
            pltpu.VMEM((4, 6, 96, 256), F32),
            pltpu.VMEM((4, 6, 48, 256), F32),
            pltpu.VMEM((4, 6, 48, 256), F32),
            pltpu.VMEM((24, 80, 768), BF16),
            pltpu.VMEM((20, 80, 768), BF16),
            pltpu.VMEM((16, 64, 256), BF16),
            pltpu.VMEM((640, 256), F32),
            pltpu.VMEM((640, 256), F32),
            pltpu.VMEM((72, 70 * 64), F32),
            pltpu.VMEM((320, 128), F32),
            pltpu.VMEM((2304, 256), BF16),
            pltpu.VMEM((2304, 256), BF16),
            pltpu.SemaphoreType.DMA((4,)),
        ],
        compiler_params=pltpu.CompilerParams(vmem_limit_bytes=VMEM),
        cost_estimate=pl.CostEstimate(flops=1 << 32, bytes_accessed=1 << 23, transcendentals=1 << 20),
    )(*strips, nat, pick, seen, *mats, left, right, act_in, flat_in)


def adjoint_kernel(
    back_in, back_rim, two_in, two_rim, one_in, one_rim, m_one_in, m_two_in, t_grad, left, right,
    grad,
    back_three, keep_two, keep_one, three, two, one, buf_a, buf_b, flat, turn, m_one, m_two, m_one_t, m_two_t, sems,
):
    load_two = copy(m_two_in, m_two, sems.at[3, 0])
    def load(inside, rim, target, first, count, pieces, sem):
        moves = [copy(inside, target.at[first : first + count], sem.at[0])]
        for k, (start, stop, to) in enumerate(pieces):
            moves.append(copy(rim.at[start:stop], target.at[to : to + stop - start], sem.at[k + 1]))
        return moves

    moves_three = load(back_in, back_rim, back_three, 8, 54, ((0, 8, 0), (8, 16, 62)), sems.at[0])
    moves_two = load(two_in, two_rim, keep_two, 8, 56, ((0, 8, 0), (8, 16, 64)), sems.at[1])
    moves_one = load(one_in, one_rim, keep_one, 8, 60, ((0, 8, 0), (16, 24, 68)), sems.at[2])
    load_one = copy(m_one_in, m_one, sems.at[3, 1])

    def turn_over(source, target):
        for tap in range(9):
            target[(8 - tap) * 256 : (9 - tap) * 256, :] = source[tap * 256 : tap * 256 + 256, :].T

    load_two.wait()
    turn_over(m_two, m_two_t)
    for move in moves_three:
        move.wait()

    def spread(s, _):
        spread_rows(three.at[s], back_three[s].astype(F32)[0:40], back_three[s + 32].astype(F32)[0:40])
        return 0

    lax.fori_loop(0, 38, spread, 0, unroll=2)
    load_one.wait()
    turn_over(m_one, m_one_t)
    for move in moves_two:
        move.wait()

    def dot_two(q, buf):
        buf[...] = three_taps(three, q * 9, 9, m_two_t)

    def finish_two(q, buf):
        for jj in range(9):
            s = q * 9 + jj
            x0 = buf[jj * 80 : jj * 80 + 40] * keep_two[s + 2]
            x1 = buf[jj * 80 + 40 : jj * 80 + 80] * keep_two[s + 34]
            spread_rows(two.at[s], x0, x1)

    pipeline((9, 9, 9, 9), dot_two, finish_two, (buf_a, buf_b))
    one[:, 48:64] = jnp.zeros((66, 16, 256), BF16)
    rest = jnp.zeros((8, 256), F32)
    for move in moves_one:
        move.wait()
    sizes = (9, 9, 8, 8)

    def dot_one(q, buf):
        buf[0 : sizes[q] * 80] = three_taps(two, sum(sizes[:q]), sizes[q], m_one_t)

    def finish_one(q, buf):
        for jj in range(sizes[q]):
            s = sum(sizes[:q]) + jj
            x0 = buf[jj * 80 : jj * 80 + 40] * keep_one[s + 6]
            x1 = buf[jj * 80 + 40 : jj * 80 + 80] * keep_one[s + 38]
            one[s, 0:48] = jnp.concatenate([x0, rest], axis=0).astype(BF16)
            one[s + 32, 0:48] = jnp.concatenate([x1, rest], axis=0).astype(BF16)

    pipeline(sizes, dot_one, finish_one, (buf_a, buf_b))
    thin_taps(t_grad[...], one, 66, flat, 0)
    image = thin_sum(flat, 64)
    rows = grad.shape[1]
    for ch in range(2):
        grad[ch] = unfold(image, ch * 4, 32, rows, left[...], right, turn)


def adjoint_pass(fields, mats, left, right):
    return pl.pallas_call(
        adjoint_kernel,
        name="adjoint_pass",
        out_shape=jax.ShapeDtypeStruct((2, left.shape[0] // 2, 128), F32),
        in_specs=[ANY] * 8 + [HERE] * 3,
        scratch_shapes=[
            pltpu.VMEM((70, 48, 256), BF16),
            pltpu.VMEM((72, 40, 256), F32),
            pltpu.VMEM((76, 40, 256), F32),
            pltpu.VMEM((38, 80, 768), BF16),
            pltpu.VMEM((36, 80, 768), BF16),
            pltpu.VMEM((66, 64, 256), BF16),
            pltpu.VMEM((720, 256), F32),
            pltpu.VMEM((720, 256), F32),
            pltpu.VMEM((72, 66 * 64), F32),
            pltpu.VMEM((256, 128), F32),
            pltpu.VMEM((2304, 256), BF16),
            pltpu.VMEM((2304, 256), BF16),
            pltpu.VMEM((2304, 256), BF16),
            pltpu.VMEM((2304, 256), BF16),
            pltpu.SemaphoreType.DMA((4, 3)),
        ],
        compiler_params=pltpu.CompilerParams(vmem_limit_bytes=VMEM),
        cost_estimate=pl.CostEstimate(flops=1 << 33, bytes_accessed=1 << 23, transcendentals=0),
    )(*fields, *mats, left, right)


def combine_kernel(basis, gram, surface, residual):
    sums = jnp.sum(gram[...], axis=0)[0:1, :]
    g = {}
    at = 0
    for i in range(4):
        for j in range(i, 4):
            g[i, j] = g[j, i] = sums[:, at : at + 1]
            at += 1

    def inner(a, b):
        total = None
        for i, ai in enumerate(a):
            for j, bj in enumerate(b):
                if ai is not None and bj is not None:
                    term = ai * bj * g[i, j]
                    total = term if total is None else total + term
        return total

    def add(a, b, scale):
        out = []
        for ai, bi in zip(a, b):
            if bi is None:
                out.append(ai)
            else:
                out.append(scale * bi if ai is None else ai + scale * bi)
        return out

    def operate(p):
        out = [None if x is None else CENTRE * x for x in p]
        if p[0] is not None:
            out = add(out, [None, p[0], None, None], RADIUS)
        if p[1] is not None:
            out = add(out, [p[1], None, p[1], None], 0.5 * RADIUS)
        if p[2] is not None:
            out = add(out, [None, p[2], None, p[2]], 0.5 * RADIUS)
        return out

    unit = jnp.ones((1, 1), F32)
    r = [unit, None, None, None]
    p = [unit, None, None, None]
    x = [None] * 4
    norm = g[0, 0]
    for step in range(3):
        image = operate(p)
        alpha = norm / inner(p, image)
        x = add(x, p, alpha)
        r = add(r, image, -alpha)
        if step < 2:
            new = inner(r, r)
            p = add(r, p, new / norm)
            norm = new
    surface[...] = x[0] * basis[0] + x[1] * basis[1] + x[2] * basis[2]
    residual[...] = r[0] * basis[0] + r[1] * basis[1] + r[2] * basis[2] + r[3] * basis[3]


def combine(basis, gram):
    shape = jax.ShapeDtypeStruct(basis.shape[1:], F32)
    return pl.pallas_call(combine_kernel, name="combine", out_shape=(shape, shape))(basis, gram)


def shards(
    base_state,
    increment,
    cotangent,
    land_sea,
    storage,
    source,
    w_first,
    w_middle_one,
    w_middle_two,
    w_last,
):
    rows = land_sea.shape[0]
    tall = rows + 2 * HALO
    gx, gy = lax.axis_size("gx"), lax.axis_size("gy")
    own, top, bottom = rows_out(base_state, increment, cotangent, land_sea, storage, source)
    above = lax.ppermute(bottom, "gy", [(i, i + 1) for i in range(gy - 1)])
    below = lax.ppermute(top, "gy", [(i + 1, i) for i in range(gy - 1)])

    e_first, e_last, e_force, e_grad, seen = one_hots()
    m_one, m_two, r_first, r_last, t_force, t_grad = fold_weights(
        w_middle_one, w_middle_two, w_first, w_last, (e_first, e_last, e_force, e_grad)
    )
    turned, nat, west, east = columns_out(own, above, below)
    far_west = lax.ppermute(east, "gx", [(i, (i + 1) % gx) for i in range(gx)])
    far_east = lax.ppermute(west, "gx", [((i + 1) % gx, i) for i in range(gx)])
    pick = decimate()
    mats = (m_one, m_two, r_first, r_last, t_force)
    back_in, two_in, one_in, act_in, flat_in = inner_pass(turned, pick, seen, mats)
    left, right = unfold_tables(tall, 36, 12, 40, 256, -4)
    back_rim, two_rim, one_rim, basis, gram = outer_pass(
        (far_west, west, east, far_east), nat, pick, seen, mats, left, right, act_in, flat_in, gx * gy
    )
    gram = lax.all_to_all(gram, ("gx", "gy"), 0, 0)
    left, right = unfold_tables(rows, 32, 0, 32, 128, 0)
    fields = (back_in, back_rim, two_in, two_rim, one_in, one_rim)
    grad = adjoint_pass(fields, (m_one, m_two, t_grad), left, right)
    surface, residual = combine(basis, gram)
    return (grad, surface, residual)


def solution(mesh):
    placed = (
        P(None, "gy", "gx"),
        P(None, "gy", "gx"),
        P("gy", "gx"),
        P("gy", "gx"),
        P("gy", "gx"),
        P("gy", "gx"),
        P(),
        P(),
        P(),
        P(),
    )
    return jax.shard_map(
        shards,
        mesh=mesh,
        in_specs=placed,
        out_specs=(P(None, "gy", "gx"), P("gy", "gx"), P("gy", "gx")),
        check_vma=False,
    )
```

```python
import functools

import jax
import jax.numpy as jnp
import numpy as np
from jax import lax
from jax.experimental import pallas as pl
from jax.experimental.pallas import tpu as pltpu
from jax.sharding import PartitionSpec as P

F32 = jnp.float32
BF16 = jnp.bfloat16
HALO = 16
CENTRE = 6.125
RADIUS = 5.875
MIB = 1024 * 1024
ANY = pl.BlockSpec(memory_space=pl.ANY)
HERE = pl.BlockSpec(memory_space=pltpu.VMEM)


def one_hots():
    first = np.zeros((16, 96, 32), np.float32)
    last = np.zeros((16, 96, 32), np.float32)
    for s in range(16):
        jj, qr, qc = s // 4, s // 2 % 2, s % 2
        for dr in range(6):
            for x in range(16):
                a, b = dr - qr, x - 2 * jj - qc
                if 0 <= a < 5 and 0 <= b < 5:
                    first[s, dr * 16 + x, a * 5 + b] = 1
                    last[s, dr * 16 + x, (4 - a) * 5 + 4 - b] = 1
    force = np.zeros((4, 72, 32), np.float32)
    grad = np.zeros((4, 2, 72, 32), np.float32)
    for p in range(4):
        pr, pc = p // 2, p % 2
        for dr in range(3):
            for dc in range(3):
                for q in range(4):
                    qr, qc = q // 2, q % 2
                    a, b = 2 * dr + pr - qr, 2 * dc + pc - qc
                    if 0 <= a < 5 and 0 <= b < 5:
                        force[p, (dr * 3 + dc) * 8 + q, a * 5 + b] = 1
                        for ch in range(2):
                            grad[p, ch, (dr * 3 + dc) * 8 + ch * 4 + q, (4 - a) * 5 + 4 - b] = 1
    seen = np.zeros((128, 1024), np.float32)
    for s in range(16):
        jj, qr, qc = s // 4, s // 2 % 2, s % 2
        seen[96 + qr * 16 + 2 + 2 * jj + qc, s * 64 : s * 64 + 64] = 1
    return [jnp.asarray(t, BF16) for t in (first, last, force, grad, seen)]


def decimate():
    table = np.zeros((128, 768), np.float32)
    for dr in range(6):
        for i in range(42):
            table[2 * i + dr + 4, dr * 128 + i] = 1
    return jnp.asarray(table, BF16)


def unfold_tables(rows, blocks, first_row, pairs, width, first_col):
    left = np.zeros((2 * rows, 256), np.float32)
    right = np.zeros((4 * pairs, width), np.float32)
    for par in range(2):
        for qr in range(2):
            for i in range(blocks):
                row = 2 * i + qr + first_row
                if 0 <= row < rows:
                    left[par * rows + row, qr * 128 + par * 64 + i] = 1
        for qc in range(2):
            for jp in range(pairs):
                col = 4 * jp + 2 * par + qc + first_col
                if -HALO <= col < 128 + HALO:
                    right[(par * 2 + qc) * pairs + jp, col % width] = 1
    return jnp.asarray(left), jnp.asarray(right)


def mm(a, b, dims=((1,), (0,))):
    return lax.dot_general(a, b, (dims, ((), ())), preferred_element_type=F32)


def exact(a, b, dims=((1,), (0,))):
    return lax.dot_general(
        a, b, (dims, ((), ())), preferred_element_type=F32, precision=lax.Precision.HIGHEST
    )


def up(x, by):
    return x if by == 0 else pltpu.roll(x, x.shape[0] - by, axis=0)


def unpack_taps(raw, stage, taps):
    for i in range(32):
        stage[i * 32 : i * 32 + 25, :] = raw[:, i * 128 : i * 128 + 128].astype(F32)
    for t in range(25):
        pairs = stage[pl.ds(t, 32, stride=32), :]
        taps[t, pl.ds(0, 32, stride=2), :] = pairs[:, 0:64]
        taps[t, pl.ds(1, 32, stride=2), :] = pairs[:, 64:128]


def fold_middle(taps, out_ref):
    zero = jnp.zeros((64, 64), F32)
    for dc in range(3):
        for dr in range(3):
            for p in range(4):
                pr, pc = p // 2, p % 2
                parts = []
                for q in range(4):
                    qr, qc = q // 2, q % 2
                    a, b = 2 * dr + pr - qr, 2 * dc + pc - qc
                    parts.append(taps[a * 5 + b] if 0 <= a < 5 and 0 <= b < 5 else zero)
                at = (dc * 3 + dr) * 256 + p * 64
                out_ref[at : at + 64, :] = jnp.concatenate(parts, axis=1).astype(BF16)


def weights_kernel(
    w_one, w_two, w_first, w_last, e_first, e_last, e_force, e_grad,
    m_one, m_two, r_first, r_last, t_force, t_grad,
    stage, taps,
):
    for k, (raw, out) in enumerate(((w_one, m_one), (w_two, m_two))):
        unpack_taps(raw, stage.at[k], taps.at[k])
        fold_middle(taps.at[k], out)
    wf = w_first[...]
    wl = w_last[...]
    pad = jnp.zeros((7, 64), BF16)
    wf = [jnp.concatenate([wf[:, c * 64 : c * 64 + 64], pad], axis=0) for c in range(2)]
    wl = jnp.concatenate([wl, pad], axis=0)
    gap = jnp.zeros((32, 128), BF16)
    for s in range(0, 16, 2):
        cols = slice(s * 64, s * 64 + 128)
        for c in range(2):
            two = [mm(e_first[s + d], wf[c]).astype(BF16) for d in range(2)]
            r_first[c * 128 : c * 128 + 96, cols] = jnp.concatenate(two, axis=1)
            r_first[c * 128 + 96 : c * 128 + 128, cols] = gap
        two = [mm(e_last[s + d], wl).astype(BF16) for d in range(2)]
        r_last[0:96, cols] = jnp.concatenate(two, axis=1)
        r_last[96:128, cols] = gap
    force, grad = [], []
    for p in range(4):
        force.append(mm(e_force[p], wl))
        grad.append(mm(e_grad[p, 0], wf[0]) + mm(e_grad[p, 1], wf[1]))
    t_force[...] = jnp.concatenate(force, axis=1).astype(BF16)
    t_grad[...] = jnp.concatenate(grad, axis=1).astype(BF16)


def fold_weights(w_one, w_two, w_first, w_last, tables):
    big = jax.ShapeDtypeStruct((2304, 256), BF16)
    return pl.pallas_call(
        weights_kernel,
        name="fold_weights",
        out_shape=(
            big, big,
            jax.ShapeDtypeStruct((256, 1024), BF16),
            jax.ShapeDtypeStruct((128, 1024), BF16),
            jax.ShapeDtypeStruct((72, 256), BF16),
            jax.ShapeDtypeStruct((72, 256), BF16),
        ),
        scratch_shapes=[pltpu.VMEM((2, 1024, 128), F32), pltpu.VMEM((2, 25, 64, 64), F32)],
        compiler_params=pltpu.CompilerParams(vmem_limit_bytes=60 * MIB),
        cost_estimate=pl.CostEstimate(flops=1 << 24, bytes_accessed=1 << 23, transcendentals=0),
    )(w_one, w_two, w_first, w_last, *tables)


def copy(source, target, sem):
    move = pltpu.make_async_copy(source, target, sem)
    move.start()
    return move


def rows_kernel(base, incr, cot, land, storage, source, own, top, bottom):
    wet = land[...].astype(F32)
    images = [base[0], base[1], incr[0], incr[1], cot[...].astype(F32) * wet, wet, storage[...], source[...]]
    rows = land.shape[0]
    for c, image in enumerate(images):
        image = image.astype(F32)
        own[c] = image
        top[c] = image[:HALO]
        bottom[c] = image[rows - HALO :]


def rows_out(*fields):
    rows, cols = fields[3].shape
    edge = jax.ShapeDtypeStruct((8, HALO, cols), F32)
    return pl.pallas_call(
        rows_kernel,
        name="rows_out",
        out_shape=(jax.ShapeDtypeStruct((8, rows, cols), F32), edge, edge),
    )(*fields)


def columns_kernel(own, above, below, images, west, east):
    rest = jnp.zeros((128 - own.shape[1] - 2 * HALO, 128), F32)
    for c in range(8):
        image = jnp.concatenate([above[c], own[c], below[c], rest], axis=0)
        flipped = image.T
        if c < 6:
            images[c] = flipped
        if c >= 5:
            images[c + 1] = image
        west[c] = flipped[:HALO]
        east[c] = flipped[128 - HALO :]


def columns_out(own, above, below):
    edge = jax.ShapeDtypeStruct((8, HALO, 128), F32)
    return pl.pallas_call(
        columns_kernel,
        name="columns_out",
        out_shape=(jax.ShapeDtypeStruct((9, 128, 128), F32), edge, edge),
        compiler_params=pltpu.CompilerParams(vmem_limit_bytes=4 * MIB),
    )(own, above, below)


def three_taps(slots, at, count, weights):
    taps = [slots[pl.ds(at + dc, count)].reshape(count * 80, 768) for dc in range(3)]
    return mm(jnp.concatenate(taps, axis=1), weights[...])


def spread_rows(slot, x0, x1):
    for dr in range(3):
        both = jnp.concatenate([up(x0, dr)[0:40], up(x1, dr)[0:40]], axis=0)
        slot[:, dr * 256 : dr * 256 + 256] = both.astype(BF16)


def thin_taps(table, slots, count, flat_ref, lane):
    for q in range(0, count, 4):
        take = min(4, count - q)
        x = slots[q : q + take].reshape(take * 64, 256)
        flat_ref[:, lane + q * 64 : lane + (q + take) * 64] = mm(table, x, ((1,), (1,)))


def thin_sum(flat_ref, outs):
    span = outs * 64
    total = None
    for dr in range(3):
        part = None
        for dc in range(3):
            tap = flat_ref[(dr * 3 + dc) * 8 : (dr * 3 + dc) * 8 + 8, dc * 64 : dc * 64 + span]
            part = tap if part is None else part + tap
        if dr:
            part = pltpu.roll(part, span - dr, axis=1)
        total = part if total is None else total + part
    return total


def unfold(image, fields, pairs, left, right, turn_ref):
    for jp in range(image.shape[1] // 128):
        turn_ref[jp * 8 : jp * 8 + 8, :] = image[:, jp * 128 : jp * 128 + 128]
    picks = []
    for f in range(fields):
        for qc in range(2):
            two = [turn_ref[pl.ds(f * 4 + qr * 2 + qc, pairs, stride=8), :] for qr in range(2)]
            picks.append(jnp.concatenate(two, axis=1))
    half = exact(left, jnp.concatenate(picks, axis=0), ((1,), (1,)))
    rows, span = half.shape[0] // 2, 2 * pairs
    parts = []
    for f in range(fields):
        two = [half[par * rows : par * rows + rows, f * span : f * span + span] for par in range(2)]
        parts.append(jnp.concatenate(two, axis=1))
    return exact(jnp.concatenate(parts, axis=0), right)


def slab(window, row, k, lhs, lhs_back):
    views = [window[c, pl.ds(row, 16), :] for c in range(6)]

    def stack(c):
        parts = [views[c][:, dr * 128 : dr * 128 + 128] for dr in range(6)]
        parts += [views[5][:, dr * 128 : dr * 128 + 128] for dr in (2, 3)]
        return jnp.concatenate(parts, axis=0).T[:48]

    slabs = [stack(c) for c in range(5)]
    base = jnp.concatenate(slabs[0:2], axis=1)
    incr = jnp.concatenate(slabs[2:4], axis=1)
    lhs[k] = jnp.concatenate([base, incr], axis=0).astype(BF16)
    lhs_back[k] = up(slabs[4], 2).astype(BF16)


def first_products(lhs, lhs_back, seen, r_first, r_last, pre, wet, back_pre, first, count):
    some = slice(first, first + count)
    x = lhs[some].reshape(count * 96, 256)
    y = lhs[some, 0:48, 0:128].reshape(count * 48, 128)
    z = lhs_back[some].reshape(count * 48, 128)
    for jj in range(4):
        lanes = slice(jj * 256, jj * 256 + 256)
        pre[jj, some] = mm(x, r_first[:, lanes]).reshape(count, 96, 256)
        wet[jj, some] = mm(y, seen[:, lanes]).reshape(count, 48, 256)
        back_pre[jj, some] = mm(z, r_last[:, lanes]).reshape(count, 48, 256)


def first_finish(k, jj, pre, wet, slot, keep):
    slope = jnp.tanh(pre[jj, k, 0:48])
    mask = wet[jj, k]
    kept = mask * (1.0 - slope * slope)
    keep[...] = up(kept, 4)[0:40]
    spread_rows(slot, mask * slope, kept * pre[jj, k, 48:96])


def second_finish(pre, mask, slot, keep):
    slope = jnp.tanh(pre[0:40])
    mask = up(mask, 1)[0:40]
    kept = mask * (1.0 - slope * slope)
    keep[...] = up(kept, 2)
    spread_rows(slot, mask * slope, kept * pre[40:80])


def third_finish(pre, mask, back_pre, slot, back):
    rest = jnp.zeros((8, 256), F32)
    slope = jnp.tanh(pre[0:40])
    kept = up(mask, 2)[0:40] * (1.0 - slope * slope)
    slot[0:48] = jnp.concatenate([kept * pre[40:80], rest], axis=0).astype(BF16)
    back[...] = kept * back_pre[0:40]


def turn_over(source, target, tap):
    target[(8 - tap) * 256 : (9 - tap) * 256, :] = source[tap * 256 : tap * 256 + 256, :].T


def inner_kernel(
    images, pick, seen_in, m_one_in, m_two_in, r_first_in, r_last_in, t_force, t_grad,
    back_out, two_out, one_out, act_out, m_one_out, m_two_out, force_out, grad_out,
    window, lhs, lhs_back, pre, wet, back_pre, act_one, act_two, tl_three,
    buf_a, buf_b, keep_one, keep_two, back_three, m_one, m_two, m_one_t, m_two_t, one, flat,
    seen, r_first, r_last, sems,
):
    tables = [
        copy(r_first_in, r_first, sems.at[2]),
        copy(seen_in, seen, sems.at[3]),
        copy(r_last_in, r_last, sems.at[4]),
    ]
    loads = [copy(m_one_in, m_one, sems.at[0]), copy(m_two_in, m_two, sems.at[1])]
    sel = pick[...]
    for c in range(6):
        window[c] = mm(images[c].astype(BF16), sel)
    tl_three[:, 48:64] = jnp.zeros((54, 16, 256), BF16)
    one[:, 48:64] = jnp.zeros((50, 16, 256), BF16)
    force_out[...] = jnp.zeros(force_out.shape, F32)
    grad_out[...] = jnp.zeros(grad_out.shape, F32)
    flat[:, 0:128] = jnp.zeros((72, 128), F32)

    def gather(chunk):
        for k in range(chunk * 5, chunk * 5 + 5):
            slab(window, k * 8, k, lhs, lhs_back)

    def products(chunk):
        first_products(lhs, lhs_back, seen, r_first, r_last, pre, wet, back_pre, chunk * 5, 5)

    def finish_one(chunk):
        for k in range(chunk * 5, chunk * 5 + 5):
            for jj in range(4):
                first_finish(k, jj, pre, wet, act_one.at[k * 4 + jj], keep_one.at[k * 4 + jj])

    gather(0)
    for table in tables:
        table.wait()
    products(0)
    gather(1)
    products(1)
    gather(2)
    finish_one(0)
    products(2)
    finish_one(1)
    for load in loads:
        load.wait()

    def wet_at(at):
        return wet[at % 4, at // 4]

    def dot_two(q, buf):
        buf[0:640] = three_taps(act_one, q * 8 + 2, 8, m_one)

    def finish_two(q, buf):
        for jj in range(8):
            k = q * 8 + jj
            second_finish(buf[jj * 80 : jj * 80 + 80], wet_at(k + 3), act_two.at[k], keep_two.at[k])
        for tap in range(q * 2, min(q * 2 + 2, 9)):
            turn_over(m_two, m_two_t, tap)

    def dot_three(q, buf):
        buf[...] = three_taps(act_two, q * 9, 9, m_two)

    def finish_three(q, buf):
        for jj in range(9):
            k = q * 9 + jj
            at = k + 4
            third_finish(
                buf[jj * 80 : jj * 80 + 80], wet_at(at), back_pre[at % 4, at // 4], tl_three.at[k], back_three.at[k]
            )
        for tap in range(q * 2, min(q * 2 + 2, 9)):
            turn_over(m_one, m_one_t, tap)
        first, last = q * 9 // 4 * 4, (q * 9 + 9) // 4 * 4 if q < 5 else 54
        thin_taps(t_force[...], tl_three.at[first:last], last - first, flat, 128 + first * 64)

    bufs = (buf_a, buf_b)
    dot_two(0, buf_a)
    finish_one(2)
    for q in range(1, 7):
        dot_two(q, bufs[q % 2])
        finish_two(q - 1, bufs[(q - 1) % 2])
    finish_two(6, buf_a)
    moves = [
        copy(m_two_t, m_two_out, sems.at[0]),
        copy(keep_one.at[4:6], one_out, sems.at[1]),
        copy(keep_two.at[0:4], two_out.at[0:4], sems.at[2]),
        copy(keep_two.at[52:56], two_out.at[4:8], sems.at[3]),
    ]
    act_out[0:2] = act_two[0:2]
    act_out[2:4] = act_two[54:56]
    dot_three(0, buf_a)
    for q in range(1, 6):
        dot_three(q, bufs[q % 2])
        finish_three(q - 1, bufs[(q - 1) % 2])
    finish_three(5, buf_b)
    moves += [
        copy(m_one_t, m_one_out, sems.at[4]),
        copy(back_three.at[0:4], back_out.at[0:4], sems.at[5]),
        copy(back_three.at[50:54], back_out.at[4:8], sems.at[6]),
    ]

    three, two = act_one, act_two
    for s in range(29):
        spread_rows(three.at[s], back_three[s], back_three[s + 25])

    def dot_back_two(q, buf):
        buf[...] = three_taps(three, q * 9, 9, m_two_t)

    def finish_back_two(q, buf):
        for jj in range(9):
            s = q * 9 + jj
            x0 = buf[jj * 80 : jj * 80 + 40] * keep_two[s + 2]
            x1 = buf[jj * 80 + 40 : jj * 80 + 80] * keep_two[s + 27]
            spread_rows(two.at[s], x0, x1)

    starts, rest = (0, 8, 16, 25), jnp.zeros((8, 256), F32)
    groups = (((0, 8), (26, 32)), ((8, 16), (32, 40)), ((16, 26), (40, 50)))

    def dot_back_one(q, buf):
        count = starts[q + 1] - starts[q]
        buf[0 : count * 80] = three_taps(two, starts[q], count, m_one_t)

    def finish_back_one(q, buf):
        for jj in range(starts[q + 1] - starts[q]):
            s = starts[q] + jj
            x0 = buf[jj * 80 : jj * 80 + 40] * keep_one[s + 6]
            x1 = buf[jj * 80 + 40 : jj * 80 + 80] * keep_one[s + 31]
            one[s, 0:48] = jnp.concatenate([x0, rest], axis=0).astype(BF16)
            one[s + 25, 0:48] = jnp.concatenate([x1, rest], axis=0).astype(BF16)
        for first, last in groups[q]:
            thin_taps(t_grad[...], one.at[first:last], last - first, flat, 128 + first * 64)

    dot_back_two(0, buf_a)
    flat[:, 128 + 54 * 64 :] = jnp.zeros((72, 128), F32)
    force_out[:, 384 : 384 + 56 * 64] = thin_sum(flat, 56)
    dot_back_two(1, buf_b)
    finish_back_two(0, buf_a)
    dot_back_two(2, buf_a)
    finish_back_two(1, buf_b)
    finish_back_two(2, buf_a)
    flat[:, 128 + 50 * 64 : 256 + 50 * 64] = jnp.zeros((72, 128), F32)
    dot_back_one(0, buf_a)
    dot_back_one(1, buf_b)
    finish_back_one(0, buf_a)
    dot_back_one(2, buf_a)
    finish_back_one(1, buf_b)
    finish_back_one(2, buf_a)
    grad_out[:, 384 : 384 + 52 * 64] = thin_sum(flat, 52)
    for move in moves:
        move.wait()


def inner_pass(images, pick, seen, mats, t_grad):
    big = jax.ShapeDtypeStruct((2304, 256), BF16)
    return pl.pallas_call(
        inner_kernel,
        name="inner_pass",
        out_shape=(
            jax.ShapeDtypeStruct((8, 40, 256), F32),
            jax.ShapeDtypeStruct((8, 40, 256), F32),
            jax.ShapeDtypeStruct((2, 40, 256), F32),
            jax.ShapeDtypeStruct((4, 80, 768), BF16),
            big,
            big,
            jax.ShapeDtypeStruct((8, 68 * 64), F32),
            jax.ShapeDtypeStruct((8, 64 * 64), F32),
        ),
        in_specs=[HERE] * 2 + [ANY] * 5 + [HERE] * 2,
        out_specs=(ANY, ANY, ANY, HERE, ANY, ANY, HERE, HERE),
        scratch_shapes=[
            pltpu.VMEM((6, 128, 768), F32),
            pltpu.VMEM((15, 96, 256), BF16),
            pltpu.VMEM((15, 48, 128), BF16),
            pltpu.VMEM((4, 15, 96, 256), F32),
            pltpu.VMEM((4, 15, 48, 256), F32),
            pltpu.VMEM((4, 15, 48, 256), F32),
            pltpu.VMEM((60, 80, 768), BF16),
            pltpu.VMEM((56, 80, 768), BF16),
            pltpu.VMEM((54, 64, 256), BF16),
            pltpu.VMEM((720, 256), F32),
            pltpu.VMEM((720, 256), F32),
            pltpu.VMEM((60, 40, 256), F32),
            pltpu.VMEM((56, 40, 256), F32),
            pltpu.VMEM((54, 40, 256), F32),
            pltpu.VMEM((2304, 256), BF16),
            pltpu.VMEM((2304, 256), BF16),
            pltpu.VMEM((2304, 256), BF16),
            pltpu.VMEM((2304, 256), BF16),
            pltpu.VMEM((50, 64, 256), BF16),
            pltpu.VMEM((72, 58 * 64), F32),
            pltpu.VMEM(seen.shape, BF16),
            pltpu.VMEM(mats[2].shape, BF16),
            pltpu.VMEM(mats[3].shape, BF16),
            pltpu.SemaphoreType.DMA((7,)),
        ],
        compiler_params=pltpu.CompilerParams(vmem_limit_bytes=60 * MIB),
        cost_estimate=pl.CostEstimate(flops=1 << 33, bytes_accessed=1 << 23, transcendentals=1 << 21),
    )(images, pick, seen, *mats, t_grad)


def outer_kernel(
    far_west, west, east, far_east, images, pick, seen_in, m_one_in, m_two_in, r_first_in, r_last_in, t_force,
    left_in, right_in, act_in, force_in,
    back_out, two_out, one_out, basis, gram,
    window, lhs, lhs_back, pre, wet, back_pre, act_one, act_two, tl_three, buf_a, buf_b, flat, turn, m_one, m_two,
    nat, left, right, image, keep_one, keep_two, back_three, seen, r_first, r_last, sems,
):
    tables = [
        copy(r_first_in, r_first, sems.at[10]),
        copy(seen_in, seen, sems.at[11]),
        copy(r_last_in, r_last, sems.at[12]),
    ]
    load_one = copy(m_one_in, m_one, sems.at[2])
    load_act = copy(act_in, act_two.at[8:12], sems.at[3])
    load_two = copy(m_two_in, m_two, sems.at[4])
    late = [
        copy(images.at[6:9, 0 : nat.shape[1]], nat, sems.at[5]),
        copy(left_in, left, sems.at[6]),
        copy(right_in, right, sems.at[7]),
        copy(force_in, image, sems.at[8]),
    ]
    sel = pick[...]
    tl_three[:, 48:64] = jnp.zeros((20, 16, 256), BF16)
    tl_three[8:12] = jnp.zeros((4, 64, 256), BF16)
    turn[...] = jnp.zeros(turn.shape, F32)
    for c in range(6):
        strips = [far_west[c], west[c], east[c], far_east[c]]
        window[c] = mm(jnp.concatenate(strips, axis=0).astype(BF16), sel)
    for k in range(6):
        slab(window, (0, 8, 16, 32, 40, 48)[k], k, lhs, lhs_back)
    for move in tables:
        move.wait()
    first_products(lhs, lhs_back, seen, r_first, r_last, pre, wet, back_pre, 0, 6)
    for k in range(6):
        for jj in range(4):
            first_finish(k, jj, pre, wet, act_one.at[k * 4 + jj], keep_one.at[k * 4 + jj])
    sends = [copy(keep_one.at[6:20], one_out, sems.at[9])]
    load_one.wait()

    def dot_two(q, buf):
        buf[...] = three_taps(act_one, (2, 14)[q], 8, m_one)

    def finish_two(q, buf):
        for jj in range(8):
            at = (3, 15)[q] + jj
            second_finish(
                buf[jj * 80 : jj * 80 + 80], wet[at % 4, at // 4], act_two.at[(0, 12)[q] + jj], keep_two.at[q * 8 + jj]
            )

    def dot_three(q, buf):
        buf[...] = three_taps(act_two, (0, 10)[q], 8, m_two)

    def finish_three(q, buf):
        for jj in range(8):
            at = (4, 14)[q] + jj
            third_finish(
                buf[jj * 80 : jj * 80 + 80], wet[at % 4, at // 4], back_pre[at % 4, at // 4],
                tl_three.at[q * 12 + jj], back_three.at[q * 8 + jj],
            )

    dot_two(0, buf_a)
    dot_two(1, buf_b)
    finish_two(0, buf_a)
    load_act.wait()
    load_two.wait()
    dot_three(0, buf_a)
    finish_two(1, buf_b)
    sends.append(copy(keep_two, two_out, sems.at[13]))
    dot_three(1, buf_b)
    finish_three(0, buf_a)
    thin_taps(t_force[...], tl_three.at[0:10], 10, flat.at[0], 0)
    finish_three(1, buf_b)
    sends.append(copy(back_three, back_out, sems.at[14]))
    thin_taps(t_force[...], tl_three.at[10:20], 10, flat.at[1], 0)
    for move in late:
        move.wait()
    image[:, 0:512] += thin_sum(flat.at[0], 8)
    image[:, 60 * 64 :] += thin_sum(flat.at[1], 8)
    tall = nat.shape[1]
    force = unfold(image[...], 1, 64, left[...], right[...], turn)
    gap = jnp.zeros((128 - 2 * HALO, 128), F32)

    def wide(c):
        rim = jnp.concatenate([far_east[c], gap, far_west[c]], axis=0).T[:tall]
        return jnp.concatenate([nat[c - 5], rim], axis=1)

    mask, storage, source = wide(5), wide(6), wide(7)
    columns = mask.shape[1]
    to_east = mask * pltpu.roll(mask, columns - 1, axis=1)
    to_west = mask * pltpu.roll(mask, 1, axis=1)
    to_north = mask * pltpu.roll(mask, tall - 1, axis=0)
    to_south = mask * pltpu.roll(mask, 1, axis=0)

    def scaled(v):
        total = storage * v + to_east * (v - pltpu.roll(v, columns - 1, axis=1))
        total = total + to_west * (v - pltpu.roll(v, 1, axis=1))
        total = total + to_north * (v - pltpu.roll(v, tall - 1, axis=0))
        total = total + to_south * (v - pltpu.roll(v, 1, axis=0))
        return (total - CENTRE * v) * (1.0 / RADIUS)

    v0 = source + mask * force
    v1 = scaled(v0)
    v2 = 2.0 * scaled(v1) - v0
    v3 = 2.0 * scaled(v2) - v1
    inner = [v[HALO : tall - HALO, 0:128] for v in (v0, v1, v2, v3)]
    for k in range(4):
        basis[k] = inner[k]
    sums = []
    for i in range(4):
        for j in range(i, 4):
            sums.append(jnp.sum(inner[i] * inner[j], axis=0, keepdims=True))
    sums.append(jnp.zeros((16 - len(sums), 128), F32))
    sums = jnp.sum(jnp.concatenate(sums, axis=0), axis=1, keepdims=True)
    row = lax.broadcasted_iota(jnp.int32, (16, 128), 0)
    lane = lax.broadcasted_iota(jnp.int32, (16, 128), 1)
    sums = jnp.sum(jnp.where(row == lane, sums, 0.0), axis=0, keepdims=True)
    gram[...] = jnp.broadcast_to(sums, gram.shape)
    for send in sends:
        send.wait()


def outer_pass(strips, images, tall, pick, seen, mats, left, right, act_in, force_in, devices):
    return pl.pallas_call(
        outer_kernel,
        name="outer_pass",
        out_shape=(
            jax.ShapeDtypeStruct((16, 40, 256), F32),
            jax.ShapeDtypeStruct((16, 40, 256), F32),
            jax.ShapeDtypeStruct((14, 40, 256), F32),
            jax.ShapeDtypeStruct((4, tall - 2 * HALO, 128), F32),
            jax.ShapeDtypeStruct((devices, 1, 128), F32),
        ),
        in_specs=[HERE, HERE, HERE, HERE, ANY, HERE, ANY, ANY, ANY, ANY, ANY, HERE, ANY, ANY, ANY, ANY],
        out_specs=(ANY, ANY, ANY, HERE, HERE),
        scratch_shapes=[
            pltpu.VMEM((6, 64, 768), F32),
            pltpu.VMEM((6, 96, 256), BF16),
            pltpu.VMEM((6, 48, 128), BF16),
            pltpu.VMEM((4, 6, 96, 256), F32),
            pltpu.VMEM((4, 6, 48, 256), F32),
            pltpu.VMEM((4, 6, 48, 256), F32),
            pltpu.VMEM((24, 80, 768), BF16),
            pltpu.VMEM((20, 80, 768), BF16),
            pltpu.VMEM((20, 64, 256), BF16),
            pltpu.VMEM((640, 256), F32),
            pltpu.VMEM((640, 256), F32),
            pltpu.VMEM((2, 72, 10 * 64), F32),
            pltpu.VMEM((512, 128), F32),
            pltpu.VMEM((2304, 256), BF16),
            pltpu.VMEM((2304, 256), BF16),
            pltpu.VMEM((3, tall, 128), F32),
            pltpu.VMEM(left.shape, F32),
            pltpu.VMEM(right.shape, F32),
            pltpu.VMEM((8, 68 * 64), F32),
            pltpu.VMEM((24, 40, 256), F32),
            pltpu.VMEM((16, 40, 256), F32),
            pltpu.VMEM((16, 40, 256), F32),
            pltpu.VMEM(seen.shape, BF16),
            pltpu.VMEM(mats[2].shape, BF16),
            pltpu.VMEM(mats[3].shape, BF16),
            pltpu.SemaphoreType.DMA((15,)),
        ],
        compiler_params=pltpu.CompilerParams(vmem_limit_bytes=60 * MIB),
        cost_estimate=pl.CostEstimate(flops=1 << 32, bytes_accessed=1 << 23, transcendentals=1 << 20),
    )(*strips, images, pick, seen, *mats, left, right, act_in, force_in)


def adjoint_kernel(
    back_in, back_rim, two_in, two_rim, one_in, one_rim, m_one_in, m_two_in, t_grad, left, right, grad_in,
    grad,
    back_three, keep_two, keep_one, three, two, one, buf_a, buf_b, flat, turn, m_one_t, m_two_t, image, sems,
):
    moves_three = [
        copy(back_rim.at[0:8], back_three.at[0, 0:8], sems.at[0]),
        copy(back_in.at[0:4], back_three.at[0, 8:12], sems.at[1]),
        copy(back_in.at[4:8], back_three.at[1, 0:4], sems.at[2]),
        copy(back_rim.at[8:16], back_three.at[1, 4:12], sems.at[3]),
        copy(m_two_in, m_two_t, sems.at[4]),
    ]
    moves_two = [
        copy(two_rim.at[2:8], keep_two.at[0, 0:6], sems.at[5]),
        copy(two_in.at[0:4], keep_two.at[0, 6:10], sems.at[6]),
        copy(two_in.at[4:8], keep_two.at[1, 0:4], sems.at[7]),
        copy(two_rim.at[8:14], keep_two.at[1, 4:10], sems.at[8]),
        copy(m_one_in, m_one_t, sems.at[9]),
    ]
    moves_one = [
        copy(one_rim.at[0:6], keep_one.at[0, 0:6], sems.at[10]),
        copy(one_in, keep_one.at[0, 6:8], sems.at[11]),
        copy(one_rim.at[6:14], keep_one.at[1], sems.at[12]),
        copy(grad_in, image, sems.at[13]),
    ]
    one[:, 48:64] = jnp.zeros((20, 16, 256), BF16)
    one[8:12] = jnp.zeros((4, 64, 256), BF16)
    for move in moves_three:
        move.wait()
    for s in range(12):
        spread_rows(three.at[s], back_three[0, s], back_three[1, s])
    buf_a[...] = three_taps(three, 0, 10, m_two_t)
    for move in moves_two:
        move.wait()
    for s in range(10):
        x0 = buf_a[s * 80 : s * 80 + 40] * keep_two[0, s]
        x1 = buf_a[s * 80 + 40 : s * 80 + 80] * keep_two[1, s]
        spread_rows(two.at[s], x0, x1)
    buf_b[...] = three_taps(two, 0, 8, m_one_t)
    rest = jnp.zeros((8, 256), F32)
    for move in moves_one:
        move.wait()
    for s in range(8):
        x0 = buf_b[s * 80 : s * 80 + 40] * keep_one[0, s]
        x1 = buf_b[s * 80 + 40 : s * 80 + 80] * keep_one[1, s]
        one[s, 0:48] = jnp.concatenate([x0, rest], axis=0).astype(BF16)
        one[s + 12, 0:48] = jnp.concatenate([x1, rest], axis=0).astype(BF16)
    thin_taps(t_grad[...], one.at[0:10], 10, flat.at[0], 0)
    thin_taps(t_grad[...], one.at[10:20], 10, flat.at[1], 0)
    image[:, 0:512] += thin_sum(flat.at[0], 8)
    image[:, 56 * 64 :] += thin_sum(flat.at[1], 8)
    rows = grad.shape[1]
    both = unfold(image[...], 2, 32, left[...], right[...], turn)
    grad[0] = both[:rows]
    grad[1] = both[rows:]


def adjoint_pass(fields, mats, left, right, grad_in):
    return pl.pallas_call(
        adjoint_kernel,
        name="adjoint_pass",
        out_shape=jax.ShapeDtypeStruct((2, left.shape[0] // 2, 128), F32),
        in_specs=[ANY] * 8 + [HERE] * 3 + [ANY],
        scratch_shapes=[
            pltpu.VMEM((2, 12, 40, 256), F32),
            pltpu.VMEM((2, 10, 40, 256), F32),
            pltpu.VMEM((2, 8, 40, 256), F32),
            pltpu.VMEM((12, 80, 768), BF16),
            pltpu.VMEM((10, 80, 768), BF16),
            pltpu.VMEM((20, 64, 256), BF16),
            pltpu.VMEM((800, 256), F32),
            pltpu.VMEM((640, 256), F32),
            pltpu.VMEM((2, 72, 10 * 64), F32),
            pltpu.VMEM((256, 128), F32),
            pltpu.VMEM((2304, 256), BF16),
            pltpu.VMEM((2304, 256), BF16),
            pltpu.VMEM((8, 64 * 64), F32),
            pltpu.SemaphoreType.DMA((14,)),
        ],
        compiler_params=pltpu.CompilerParams(vmem_limit_bytes=60 * MIB),
        cost_estimate=pl.CostEstimate(flops=1 << 33, bytes_accessed=1 << 23, transcendentals=0),
    )(*fields, *mats, left, right, grad_in)


def combine_kernel(basis, gram, surface, residual):
    sums = jnp.sum(gram[...], axis=0)
    g = {}
    at = 0
    for i in range(4):
        for j in range(i, 4):
            g[i, j] = g[j, i] = sums[:, at : at + 1]
            at += 1

    def inner(a, b):
        total = None
        for i, ai in enumerate(a):
            for j, bj in enumerate(b):
                if ai is not None and bj is not None:
                    term = ai * bj * g[i, j]
                    total = term if total is None else total + term
        return total

    def add(a, b, scale):
        out = []
        for ai, bi in zip(a, b):
            if bi is None:
                out.append(ai)
            else:
                out.append(scale * bi if ai is None else ai + scale * bi)
        return out

    def operate(p):
        out = [None if x is None else CENTRE * x for x in p]
        if p[0] is not None:
            out = add(out, [None, p[0], None, None], RADIUS)
        if p[1] is not None:
            out = add(out, [p[1], None, p[1], None], 0.5 * RADIUS)
        if p[2] is not None:
            out = add(out, [None, p[2], None, p[2]], 0.5 * RADIUS)
        return out

    unit = jnp.ones((1, 1), F32)
    r = [unit, None, None, None]
    p = [unit, None, None, None]
    x = [None] * 4
    norm = g[0, 0]
    for step in range(3):
        image = operate(p)
        alpha = norm / inner(p, image)
        x = add(x, p, alpha)
        r = add(r, image, -alpha)
        if step < 2:
            new = inner(r, r)
            p = add(r, p, new / norm)
            norm = new
    surface[...] = x[0] * basis[0] + x[1] * basis[1] + x[2] * basis[2]
    residual[...] = r[0] * basis[0] + r[1] * basis[1] + r[2] * basis[2] + r[3] * basis[3]


def combine(basis, gram):
    shape = jax.ShapeDtypeStruct(basis.shape[1:], F32)
    return pl.pallas_call(
        combine_kernel, name="combine", out_shape=(shape, shape),
        compiler_params=pltpu.CompilerParams(vmem_limit_bytes=4 * MIB),
    )(basis, gram)


def shards(
    base_state,
    increment,
    cotangent,
    land_sea,
    storage,
    source,
    w_first,
    w_middle_one,
    w_middle_two,
    w_last,
):
    rows = land_sea.shape[0]
    tall = rows + 2 * HALO
    gx, gy = lax.axis_size("gx"), lax.axis_size("gy")
    own, top, bottom = rows_out(base_state, increment, cotangent, land_sea, storage, source)
    above = lax.ppermute(bottom, "gy", [(i, i + 1) for i in range(gy - 1)])
    below = lax.ppermute(top, "gy", [(i + 1, i) for i in range(gy - 1)])

    e_first, e_last, e_force, e_grad, seen = one_hots()
    m_one, m_two, r_first, r_last, t_force, t_grad = fold_weights(
        w_middle_one, w_middle_two, w_first, w_last, (e_first, e_last, e_force, e_grad)
    )
    images, west, east = columns_out(own, above, below)
    far_west = lax.ppermute(east, "gx", [(i, (i + 1) % gx) for i in range(gx)])
    far_east = lax.ppermute(west, "gx", [((i + 1) % gx, i) for i in range(gx)])
    pick = decimate()
    mats = (m_one, m_two, r_first, r_last, t_force)
    back_in, two_in, one_in, act_in, m_one_t, m_two_t, force_in, grad_in = inner_pass(images, pick, seen, mats, t_grad)
    left, right = unfold_tables(tall, 36, 12, 64, 256, -4)
    back_rim, two_rim, one_rim, basis, gram = outer_pass(
        (far_west, west, east, far_east), images, tall, pick, seen, mats, left, right, act_in, force_in, gx * gy
    )
    gram = lax.all_to_all(gram, ("gx", "gy"), 0, 0)
    left, right = unfold_tables(rows, 32, 0, 32, 128, 0)
    fields = (back_in, back_rim, two_in, two_rim, one_in, one_rim)
    grad = adjoint_pass(fields, (m_one_t, m_two_t, t_grad), left, right, grad_in)
    surface, residual = combine(basis, gram)
    return (grad, surface, residual)


def solution(mesh):
    placed = (
        P(None, "gy", "gx"),
        P(None, "gy", "gx"),
        P("gy", "gx"),
        P("gy", "gx"),
        P("gy", "gx"),
        P("gy", "gx"),
        P(),
        P(),
        P(),
        P(),
    )
    return jax.shard_map(
        shards,
        mesh=mesh,
        in_specs=placed,
        out_specs=(P(None, "gy", "gx"), P("gy", "gx"), P("gy", "gx")),
        check_vma=False,
    )
```
